32 devices in a mesh: gx: 4 (over y, core), gy: 8 (over z, x).
Axes of the slice: x: 2, y: 2, z: 4, core: 2. Of those that a mesh axis runs over, the one named last changes fastest.
Arguments:
- tokens: bfloat16 [10960, 8, 128], P('gx', 'gy'), may hold values from -6 to 6
- project_in: bfloat16 [1024, 3, 1024], P('gy', None, 'gx'), may hold values from -0.1875 to 0.1875
- query_bias: float32 [1024], P('gx'), may hold values from -3 to 3
- value_bias: float32 [1024], P('gx'), may hold values from -3 to 3
- project_out: bfloat16 [1024, 1024], P('gx', 'gy'), may hold values from -0.75 to 0.75
- output_bias: float32 [1024], P('gy'), may hold values from -2 to 2
- attention_scale: float32 [1024], P('gy'), may hold values from 0.5 to 2
- first_norm_gain: float32 [1024], P('gy'), may hold values from 0.1 to 1.9
- first_norm_bias: float32 [1024], P('gy'), may hold values from -2 to 2
- second_norm_gain: float32 [1024], P('gy'), may hold values from 0.1 to 1.9
- second_norm_bias: float32 [1024], P('gy'), may hold values from -2 to 2
- expand_weight: bfloat16 [1024, 4096], P('gy', 'gx'), may hold values from -0.1875 to 0.1875
- expand_bias: float32 [4096], P('gx'), may hold values from -3 to 3
- shrink_weight: bfloat16 [4096, 1024], P('gx', 'gy'), may hold values from -0.09375 to 0.09375
- shrink_bias: float32 [1024], P('gy'), may hold values from -2 to 2
- feedforward_scale: float32 [1024], P('gy'), may hold values from 0.5 to 2
- cotangent: bfloat16 [10960, 8, 128], P('gx', 'gy'), may hold values from -6 to 6
Outputs:
- block_output: bfloat16 [10960, 8, 128], P('gx', 'gy')
- input_gradient: float32 [10960, 8, 128], P('gx', 'gy')
- project_in_grad: float32 [1024, 3, 1024], P('gy', None, 'gx')
- query_bias_grad: float32 [1024], P('gx')
- value_bias_grad: float32 [1024], P('gx')
- project_out_grad: float32 [1024, 1024], P('gx', 'gy')
- output_bias_grad: float32 [1024], P('gy')
- attention_scale_grad: float32 [1024], P('gy')
- first_gain_grad: float32 [1024], P('gy')
- first_shift_grad: float32 [1024], P('gy')
- second_gain_grad: float32 [1024], P('gy')
- second_shift_grad: float32 [1024], P('gy')
- expand_weight_grad: float32 [1024, 4096], P('gy', 'gx')
- expand_bias_grad: float32 [4096], P('gx')
- shrink_weight_grad: float32 [4096, 1024], P('gx', 'gy')
- shrink_bias_grad: float32 [1024], P('gy')
- feedforward_scale_grad: float32 [1024], P('gy')
The draws below stay inside these ranges and needn't reach their ends.
All inputs are finite; a program needn't handle non-finite values.
Results may differ from the reference program's by a relative error of at most 0.012.
The reference program's roundings to bfloat16 on the way count: a program that leaves them out, or rounds other values in their place, can miss the bound.
Values may be sent and summed in bfloat16 or wider, within the bound.
No kernel may reach another device: no remote copies, remote signals or barrier semaphores. Data moves between devices by JAX's collectives and lax.ppermute only.
A program may use at most 512 MiB of HBM per device.

```python
import math
import jax
import jax.numpy as jnp
from jax import lax

D = 1024
HEADS = 16
HEAD_DIM = 64
FF = 4096
SEQ = 1370
IMAGES = 8
TOKENS = 10960
PACK = 1
N_GY = 8


def levels(stream_key, extent, shards, least, high):
    level = 1.0
    for position, blocks in shards:
        steps = jax.random.uniform(jax.random.fold_in(jax.random.fold_in(stream_key, 6), position), (blocks,), jnp.float32, least / len(shards), high / len(shards))
        level = level * jnp.repeat(jnp.exp(steps), extent[position] // blocks).reshape((-1,) + (1,) * (len(extent) - 1 - position))
    return level


def centred(rng, shape, width, most, pieces=(), held_as=jnp.bfloat16):
    level = levels(rng, shape, pieces, -0.22, 0.18) if pieces else 1.0
    entries = jax.random.normal(rng, shape, jnp.float32) * width * level
    return jnp.minimum(jnp.maximum(entries, -most), most).astype(held_as)


def setup_inputs(seed: int = 0) -> dict:
    arg_keys = jax.random.split(jax.random.key(seed), 18)
    return {
        "tokens": centred(arg_keys[0], (TOKENS // PACK, N_GY, PACK * D // N_GY), 1.0, 6.0, ((0, 4), (1, 8))),
        "project_in": centred(arg_keys[1], (D, 3, D), D ** -0.5, 0.1875, ((0, 8), (2, 4))),
        "query_bias": centred(arg_keys[2], (D,), 0.5, 3.0, ((0, 4),), jnp.float32),
        "value_bias": centred(arg_keys[3], (D,), 0.5, 3.0, ((0, 4),), jnp.float32),
        "project_out": centred(arg_keys[4], (D, D), (D // 16) ** -0.5, 0.75, ((0, 4), (1, 8))),
        "output_bias": centred(arg_keys[5], (D,), 0.3, 2.0, ((0, 8),), jnp.float32),
        "attention_scale": jnp.clip(jnp.exp(math.log(2.0) - 1.3862944 * jax.random.uniform(arg_keys[6], (D,), jnp.float32) ** levels(arg_keys[6], (D,), ((0, 8),), -0.2, 0.2)), 0.5, 2.0),
        "first_norm_gain": jnp.clip(1.0 + 0.18 * jax.random.normal(arg_keys[7], (D,), jnp.float32), 0.1, 1.9),
        "first_norm_bias": centred(arg_keys[8], (D,), 0.3, 2.0, ((0, 8),), jnp.float32),
        "second_norm_gain": jnp.clip(1.0 + 0.18 * jax.random.normal(arg_keys[9], (D,), jnp.float32), 0.1, 1.9),
        "second_norm_bias": centred(arg_keys[10], (D,), 0.3, 2.0, ((0, 8),), jnp.float32),
        "expand_weight": centred(arg_keys[11], (D, FF), D ** -0.5, 0.1875, ((0, 8), (1, 4))),
        "expand_bias": centred(arg_keys[12], (FF,), 0.5, 3.0, ((0, 4),), jnp.float32),
        "shrink_weight": centred(arg_keys[13], (FF, D), FF ** -0.5, 0.09375, ((0, 4), (1, 8))),
        "shrink_bias": centred(arg_keys[14], (D,), 0.3, 2.0, ((0, 8),), jnp.float32),
        "feedforward_scale": jnp.clip(jnp.exp(math.log(2.0) - 1.3862944 * jax.random.uniform(arg_keys[15], (D,), jnp.float32) ** levels(arg_keys[15], (D,), ((0, 8),), -0.2, 0.2)), 0.5, 2.0),
        "cotangent": centred(arg_keys[16], (TOKENS // PACK, N_GY, PACK * D // N_GY), 1.0, 6.0, ((0, 4), (1, 8))),
    }


@jax.custom_vjp
def low(v):
    return lax.optimization_barrier(v.astype(jnp.bfloat16)).astype(jnp.float32)

@jax.custom_vjp
def low_back(v):
    return v

def low_keep(v):
    return (low(v), None)

def low_pass(kept, grad):
    return (grad,)

def back_keep(v):
    return (v, None)

def back_low(kept, grad):
    return (low(grad),)
low.defvjp(low_keep, low_pass)
low_back.defvjp(back_keep, back_low)

def unpack(packed):
    slice_width = D // N_GY
    return packed.reshape(TOKENS // PACK, N_GY, PACK, slice_width).transpose(0, 2, 1, 3).reshape(TOKENS, D)

def repack(flat):
    slice_width = D // N_GY
    return flat.reshape(TOKENS // PACK, PACK, N_GY, slice_width).transpose(0, 2, 1, 3).reshape(TOKENS // PACK, N_GY, PACK * slice_width)

def layer_norm(values, gain, shift):
    center = lax.optimization_barrier(jnp.mean(values, axis=-1, keepdims=True))
    spread = lax.optimization_barrier(jnp.mean(values * values, axis=-1, keepdims=True)) - center * center
    return (values - center) * lax.rsqrt(spread + 1e-06) * gain + shift

def attend(parts):
    query, keys, values = parts
    scores = jnp.einsum('qhd,khd->hqk', query, keys, precision=lax.Precision.HIGHEST) * HEAD_DIM ** (-0.5)
    scores = low_back(scores)
    weights = low(jax.nn.softmax(scores, axis=-1))
    return jnp.einsum('hqk,khd->qhd', weights, values, precision=lax.Precision.HIGHEST)

def block(input_tokens, project_in, query_bias, value_bias, project_out, output_bias, attention_scale, first_norm_gain, first_norm_bias, second_norm_gain, second_norm_bias, expand_weight, expand_bias, shrink_weight, shrink_bias, feedforward_scale):
    rows = input_tokens.shape[0]
    first_normed = low(layer_norm(input_tokens, first_norm_gain, first_norm_bias))
    mixed = jnp.dot(first_normed, project_in.reshape(D, 3 * D), precision=lax.Precision.HIGHEST).reshape(rows, 3, D)
    query = low_back(low(mixed[:, 0] + query_bias))
    keys = low_back(low(mixed[:, 1]))
    values = low_back(low(mixed[:, 2] + value_bias))
    shape_four = (IMAGES, SEQ, HEADS, HEAD_DIM)
    attended = lax.map(jax.checkpoint(attend), (query.reshape(shape_four), keys.reshape(shape_four), values.reshape(shape_four)))
    attended = low_back(low(attended.reshape(rows, D)))
    branch_a = low_back(jnp.dot(attended, project_out, precision=lax.Precision.HIGHEST)) + output_bias
    middle_residual = input_tokens + attention_scale * branch_a
    second_normed = low(layer_norm(middle_residual, second_norm_gain, second_norm_bias))
    preact = low_back(jnp.dot(second_normed, expand_weight, precision=lax.Precision.HIGHEST) + expand_bias)
    hidden = low(jax.nn.gelu(preact, approximate=False))
    branch_b = low_back(jnp.dot(hidden, shrink_weight, precision=lax.Precision.HIGHEST)) + shrink_bias
    return middle_residual + feedforward_scale * branch_b

def reference(tokens, project_in, query_bias, value_bias, project_out, output_bias, attention_scale, first_norm_gain, first_norm_bias, second_norm_gain, second_norm_bias, expand_weight, expand_bias, shrink_weight, shrink_bias, feedforward_scale, cotangent):
    primals = tuple((item.astype(jnp.float32) for item in (unpack(tokens), project_in, query_bias, value_bias, project_out, output_bias, attention_scale, first_norm_gain, first_norm_bias, second_norm_gain, second_norm_bias, expand_weight, expand_bias, shrink_weight, shrink_bias, feedforward_scale)))
    output, pullback = jax.vjp(block, *primals)
    grads = pullback(unpack(cotangent).astype(jnp.float32))
    return (repack(output.astype(jnp.bfloat16)), repack(grads[0]), grads[1], grads[2], grads[3], grads[4], grads[5], grads[6], grads[7], grads[8], grads[9], grads[10], grads[11], grads[12], grads[13], grads[14], grads[15])
```

```python
import jax
import jax.numpy as jnp
from jax import lax
from jax.sharding import PartitionSpec as P

D = 1024
HEAD_DIM = 64
SEQ = 1370
SCALE = HEAD_DIM ** (-0.5)
LOW = jnp.bfloat16
WIDE = jnp.float32


def swap(values, axis, bit):
    size = lax.axis_size(axis)
    return lax.ppermute(values, axis, [(k, k ^ bit) for k in range(size)])


def gather_rows(values):
    bit = lax.axis_size("gx") // 2
    while bit:
        values = jnp.concatenate((values, swap(values, "gx", bit)), axis=0)
        bit //= 2
    return values


def slot_blocks(count):
    order = [0]
    bit = count // 2
    while bit:
        order = order + [k ^ bit for k in order]
        bit //= 2
    return order


def scatter_rows(partial):
    bit = 1
    while bit < lax.axis_size("gx"):
        half = partial.shape[0] // 2
        received = swap(partial[half:].astype(LOW), "gx", bit)
        partial = partial[:half] + received.astype(WIDE)
        bit *= 2
    return partial


def owner_pairs(nx, ny):
    images = ny // nx
    return [
        (i * ny + h * nx + q, q * ny + i * images + h)
        for i in range(nx)
        for h in range(images)
        for q in range(nx)
    ]


def to_owner(values, block):
    nx, ny = lax.axis_size("gx"), lax.axis_size("gy")
    width = D // ny
    images = values.reshape(-1, SEQ, width)
    images = jnp.pad(images, ((0, 0), (0, nx * block - SEQ), (0, 0)))
    blocks = images.reshape(ny, block, width)
    blocks = lax.all_to_all(blocks, "gy", split_axis=0, concat_axis=0, tiled=True)
    blocks = lax.ppermute(blocks, ("gx", "gy"), owner_pairs(nx, ny))
    return blocks.transpose(1, 0, 2).reshape(block, D)


def from_owner(values, packed_shape):
    nx, ny = lax.axis_size("gx"), lax.axis_size("gy")
    width = D // ny
    block = values.shape[0]
    blocks = values.reshape(block, ny, width).transpose(1, 0, 2)
    blocks = lax.ppermute(blocks, ("gx", "gy"), [(b, a) for a, b in owner_pairs(nx, ny)])
    blocks = lax.all_to_all(blocks, "gy", split_axis=0, concat_axis=0, tiled=True)
    return blocks.reshape(ny // nx, nx * block, width)[:, :SEQ].reshape(packed_shape)


def norm_forward(values, gain, shift):
    center = jnp.mean(values, axis=1, keepdims=True)
    spread = jnp.mean(values * values, axis=1, keepdims=True) - center * center
    rstd = lax.rsqrt(spread + 1e-06)
    normed = (values - center) * rstd
    return (normed * gain + shift).astype(LOW), normed, rstd


def norm_backward(grad, gain, normed, rstd):
    scaled = grad * gain
    total = jnp.mean(scaled, axis=1, keepdims=True)
    along = jnp.mean(scaled * normed, axis=1, keepdims=True)
    return rstd * (scaled - total - normed * along)


def times(left, right):
    return jnp.dot(left, right, preferred_element_type=WIDE)


def times_t(left, right):
    return lax.dot_general(left, right, (((1,), (1,)), ((), ())), preferred_element_type=WIDE)


def inner_rows(left, right):
    return lax.dot_general(left, right, (((0,), (0,)), ((), ())), preferred_element_type=WIDE)


def gelu_exact(values):
    return jax.nn.gelu(values, approximate=False)


def heads_of(values):
    return values.reshape(values.shape[0], -1, HEAD_DIM)


def attend_forward(query, keys, values, bias):
    scores = jnp.einsum("qhd,khd->hqk", heads_of(query), heads_of(keys), preferred_element_type=WIDE)
    scores = scores * SCALE + bias
    peak = jnp.max(scores, axis=-1, keepdims=True)
    raised = jnp.exp(scores - peak)
    total = jnp.sum(raised, axis=-1, keepdims=True)
    weights = (raised / total).astype(LOW)
    attended = jnp.einsum("hqk,khd->qhd", weights, heads_of(values), preferred_element_type=WIDE)
    return attended.astype(LOW).reshape(query.shape), peak + jnp.log(total)


def attend_backward(query, keys, values, grad_out, log_total, bias):
    q, k, v, g = heads_of(query), heads_of(keys), heads_of(values), heads_of(grad_out)
    scores = jnp.einsum("qhd,khd->hqk", q, k, preferred_element_type=WIDE) * SCALE + bias
    probs = jnp.exp(scores - log_total)
    grad_probs = jnp.einsum("qhd,khd->hqk", g, v, preferred_element_type=WIDE)
    grad_scores = (
        probs * (grad_probs - jnp.sum(probs * grad_probs, axis=-1, keepdims=True))
    ).astype(LOW)
    grad_query = jnp.einsum("hqk,khd->qhd", grad_scores, k, preferred_element_type=WIDE) * SCALE
    grad_keys = jnp.einsum("hqk,qhd->khd", grad_scores, q, preferred_element_type=WIDE) * SCALE
    grad_values = jnp.einsum("hqk,qhd->khd", probs.astype(LOW), g, preferred_element_type=WIDE)
    return tuple(item.astype(LOW).reshape(query.shape) for item in (grad_query, grad_keys, grad_values))


def token_sums(vectors):
    flat = vectors.reshape(vectors.shape[0], lax.axis_size("gy"), -1)
    flat = flat.transpose(1, 0, 2)
    bit = lax.axis_size("gy") // 2
    place = lax.axis_index("gy")
    while bit:
        half = flat.shape[0] // 2
        upper = (place & bit) != 0
        kept = jnp.where(upper, flat[half:], flat[:half])
        sent = jnp.where(upper, flat[:half], flat[half:])
        flat = kept + swap(sent, "gy", bit)
        bit //= 2
    flat = flat[0]
    bit = 1
    while bit < lax.axis_size("gx"):
        flat = flat + swap(flat, "gx", bit)
        bit *= 2
    return flat


def image_sums(vector):
    bit = 1
    while bit < lax.axis_size("gy"):
        vector = vector + swap(vector, "gy", bit)
        bit *= 2
    return vector


def on_device(
    tokens,
    project_in,
    query_bias,
    value_bias,
    project_out,
    output_bias,
    attention_scale,
    first_norm_gain,
    first_norm_bias,
    second_norm_gain,
    second_norm_bias,
    expand_weight,
    expand_bias,
    shrink_weight,
    shrink_bias,
    feedforward_scale,
    cotangent,
):
    nx, ny = lax.axis_size("gx"), lax.axis_size("gy")
    head_cols = project_out.shape[0]
    hidden_cols = expand_weight.shape[1]
    packed_shape = tokens.shape
    block = -(-SEQ // (nx * 16)) * 16
    column = jnp.arange(block)
    bias = jnp.concatenate(
        [
            jnp.where((lax.axis_index("gx") ^ k) * block + column < SEQ, 0.0, -1e30)
            for k in slot_blocks(nx)
        ]
    ).astype(WIDE)

    small = jnp.stack(
        (
            output_bias,
            attention_scale,
            first_norm_gain,
            first_norm_bias,
            second_norm_gain,
            second_norm_bias,
            shrink_bias,
            feedforward_scale,
        )
    )
    small = lax.all_gather(small, "gy", axis=1, tiled=True)
    out_shift, attn_scale, gain_one, shift_one, gain_two, shift_two, shrink_shift, ff_scale = [
        small[k] for k in range(8)
    ]
    inputs = to_owner(tokens, block).astype(WIDE)
    weight_in = lax.all_gather(project_in.reshape(-1, 3 * head_cols), "gy", axis=0, tiled=True)
    later = jnp.concatenate((project_out.T, expand_weight, shrink_weight.T), axis=1)
    later = lax.all_gather(later, "gy", axis=0, tiled=True)
    weight_out = later[:, :head_cols]
    weight_expand = later[:, head_cols : head_cols + hidden_cols]
    weight_shrink = later[:, head_cols + hidden_cols :]

    first, first_hat, first_rstd = norm_forward(inputs, gain_one, shift_one)
    first_all = gather_rows(first)
    mixed = times(first_all, weight_in)
    query = (mixed[:, :head_cols] + query_bias).astype(LOW)
    keys = mixed[:, head_cols : 2 * head_cols].astype(LOW)
    values = (mixed[:, 2 * head_cols :] + value_bias).astype(LOW)
    attended, log_total = attend_forward(query, keys, values, bias)

    grad = to_owner(cotangent, block).astype(WIDE)
    grad_b = grad * ff_scale
    grad_b_all = gather_rows(grad_b.astype(LOW))

    branch_a = scatter_rows(times_t(attended, weight_out)) + out_shift
    middle = inputs + attn_scale * branch_a
    second, second_hat, second_rstd = norm_forward(middle, gain_two, shift_two)
    second_all = gather_rows(second)
    preact = times(second_all, weight_expand) + expand_bias
    hidden = gelu_exact(preact).astype(LOW)
    grad_hidden = times(grad_b_all, weight_shrink)
    unused, gelu_pull = jax.vjp(gelu_exact, preact)
    grad_pre_wide = gelu_pull(grad_hidden)[0]
    grad_pre = grad_pre_wide.astype(LOW)
    grad_second = scatter_rows(times_t(grad_pre, weight_expand))
    branch_b = scatter_rows(times_t(hidden, weight_shrink)) + shrink_shift
    block_output = from_owner((middle + ff_scale * branch_b).astype(LOW), packed_shape)

    shrink_grad = inner_rows(grad_b_all, hidden)
    expand_grad = inner_rows(second_all, grad_pre)
    wide_grads = jnp.concatenate((shrink_grad, expand_grad), axis=1).astype(LOW)
    wide_grads = lax.psum_scatter(wide_grads, "gy", scatter_dimension=0, tiled=True).astype(WIDE)

    grad_middle = grad + norm_backward(grad_second, gain_two, second_hat, second_rstd)
    grad_a = grad_middle * attn_scale
    grad_a_all = gather_rows(grad_a.astype(LOW))
    grad_attended = times(grad_a_all, weight_out).astype(LOW)
    grad_query, grad_keys, grad_values = attend_backward(
        query, keys, values, grad_attended, log_total, bias
    )
    grad_mixed = jnp.concatenate((grad_query, grad_keys, grad_values), axis=1)
    grad_first = scatter_rows(times_t(grad_mixed, weight_in))
    input_gradient = grad_middle + norm_backward(grad_first, gain_one, first_hat, first_rstd)
    input_gradient = from_owner(input_gradient.astype(LOW), packed_shape).astype(WIDE)

    out_grad = inner_rows(grad_a_all, attended)
    in_grad = inner_rows(first_all, grad_mixed)
    head_grads = jnp.concatenate((out_grad, in_grad), axis=1).astype(LOW)
    head_grads = lax.psum_scatter(head_grads, "gy", scatter_dimension=0, tiled=True).astype(WIDE)

    sums = token_sums(
        jnp.stack(
            [
                jnp.sum(item, axis=0)
                for item in (
                    grad_a,
                    grad_middle * branch_a,
                    grad_first * first_hat,
                    grad_first,
                    grad_second * second_hat,
                    grad_second,
                    grad_b,
                    grad * branch_b,
                )
            ]
        )
    )
    biases = image_sums(
        jnp.concatenate(
            (
                jnp.sum(grad_query.astype(WIDE), axis=0),
                jnp.sum(grad_values.astype(WIDE), axis=0),
                jnp.sum(grad_pre.astype(WIDE), axis=0),
            )
        )
    )
    return (
        block_output,
        input_gradient,
        head_grads[:, head_cols:].reshape(-1, 3, head_cols),
        biases[:head_cols],
        biases[head_cols : 2 * head_cols],
        head_grads[:, :head_cols].T,
        sums[0],
        sums[1],
        sums[2],
        sums[3],
        sums[4],
        sums[5],
        wide_grads[:, hidden_cols:],
        biases[2 * head_cols :],
        wide_grads[:, :hidden_cols].T,
        sums[6],
        sums[7],
    )


def solution(mesh):
    rows = P("gx", "gy", None)
    wide, heads = P("gy"), P("gx")
    placed = (
        rows, P("gy", None, "gx"), heads, heads, P("gx", "gy"), wide, wide, wide, wide, wide, wide,
        P("gy", "gx"), heads, P("gx", "gy"), wide, wide, rows,
    )
    results = (
        rows, rows, P("gy", None, "gx"), heads, heads, P("gx", "gy"), wide, wide, wide, wide, wide,
        wide, P("gy", "gx"), heads, P("gx", "gy"), wide, wide,
    )
    return jax.shard_map(
        on_device, mesh=mesh, in_specs=placed, out_specs=results, check_vma=False
    )
```

```python
import math

import jax
import jax.numpy as jnp
from jax import lax
from jax.experimental import pallas as pl
from jax.experimental.pallas import tpu as pltpu
from jax.sharding import PartitionSpec as P

D = 1024
HEAD_DIM = 64
SEQ = 1370
SCALE = HEAD_DIM ** (-0.5)
LOW = jnp.bfloat16
WIDE = jnp.float32


def swap(values, axis, bit):
    size = lax.axis_size(axis)
    return lax.ppermute(values, axis, [(k, k ^ bit) for k in range(size)])


def gather_rows(values):
    bit = lax.axis_size("gx") // 2
    while bit:
        values = jnp.concatenate((values, swap(values, "gx", bit)), axis=0)
        bit //= 2
    return values


def slot_blocks(count):
    order = [0]
    bit = count // 2
    while bit:
        order = order + [k ^ bit for k in order]
        bit //= 2
    return order


def scatter_rows(partial):
    bit = 1
    while bit < lax.axis_size("gx"):
        half = partial.shape[0] // 2
        received = swap(partial[half:].astype(LOW), "gx", bit)
        partial = partial[:half] + received.astype(WIDE)
        bit *= 2
    return partial


def reversed_bits(value, count):
    turned = 0
    while count > 1:
        turned = turned * 2 + value % 2
        value //= 2
        count //= 2
    return turned


def owner_pairs(nx, ny):
    return [
        (i * ny + h * nx + q, reversed_bits(q, nx) * ny + h * nx + reversed_bits(i, nx))
        for i in range(nx)
        for h in range(ny // nx)
        for q in range(nx)
    ]


def cut_rows(values, block):
    nx, ny = lax.axis_size("gx"), lax.axis_size("gy")
    images = values.reshape(ny // nx, SEQ, D // ny)
    images = jnp.pad(images, ((0, 0), (0, nx * block - SEQ), (0, 0)))
    parts = images.reshape(ny // nx, nx, block, D // ny)
    parts = jnp.stack([parts[:, reversed_bits(q, nx)] for q in range(nx)], axis=1)
    parts = parts.reshape(ny, block, D // ny)
    return lax.all_to_all(parts, "gy", split_axis=0, concat_axis=0, tiled=True)


def to_owner(parts):
    nx, ny = lax.axis_size("gx"), lax.axis_size("gy")
    parts = lax.ppermute(parts, ("gx", "gy"), owner_pairs(nx, ny))
    return parts.transpose(1, 0, 2).reshape(parts.shape[1], D)


def leave_owner(values):
    nx, ny = lax.axis_size("gx"), lax.axis_size("gy")
    parts = values.reshape(values.shape[0], ny, D // ny).transpose(1, 0, 2)
    return lax.ppermute(parts, ("gx", "gy"), [(b, a) for a, b in owner_pairs(nx, ny)])


def join_rows(parts, packed_shape):
    nx, ny = lax.axis_size("gx"), lax.axis_size("gy")
    block = parts.shape[1]
    parts = lax.all_to_all(parts, "gy", split_axis=0, concat_axis=0, tiled=True)
    parts = parts.reshape(ny // nx, nx, block, D // ny)
    parts = jnp.stack([parts[:, reversed_bits(q, nx)] for q in range(nx)], axis=1)
    return parts.reshape(ny // nx, nx * block, D // ny)[:, :SEQ].reshape(packed_shape)


def norm_forward(values, gain, shift):
    center = jnp.mean(values, axis=1, keepdims=True)
    spread = jnp.mean(values * values, axis=1, keepdims=True) - center * center
    rstd = lax.rsqrt(spread + 1e-06)
    normed = (values - center) * rstd
    return (normed * gain + shift).astype(LOW), normed, rstd


def norm_backward(grad, gain, normed, rstd):
    scaled = grad * gain
    total = jnp.mean(scaled, axis=1, keepdims=True)
    along = jnp.mean(scaled * normed, axis=1, keepdims=True)
    return rstd * (scaled - total - normed * along)


def times(left, right):
    return jnp.dot(left, right, preferred_element_type=WIDE)


def times_t(left, right):
    return lax.dot_general(left, right, (((1,), (1,)), ((), ())), preferred_element_type=WIDE)


def inner_rows(left, right):
    return lax.dot_general(left, right, (((0,), (0,)), ((), ())), preferred_element_type=WIDE)


def lane_blocks(size):
    return [(start, min(256, size - start)) for start in range(0, size, 256)]


def with_row(head, row):
    return jnp.concatenate((head, row), axis=0)


def attend_forward_body(q_ref, k_ref, v_ref, mask_ref, ones_ref, low_ref, wide_ref, log_ref):
    keys = with_row(k_ref[...], mask_ref[...]).T
    query = with_row((q_ref[...].astype(WIDE) * SCALE).astype(LOW), ones_ref[...])
    values = with_row(v_ref[...], ones_ref[...])
    for start, size in lane_blocks(query.shape[1]):
        lanes = slice(start, start + size)
        scores = jnp.dot(keys, query[:, lanes], preferred_element_type=WIDE)
        peak = jnp.max(scores, axis=0, keepdims=True)
        raised = jnp.exp(scores - peak).astype(LOW)
        mixed = jnp.dot(values, raised, preferred_element_type=WIDE)
        total = mixed[HEAD_DIM : HEAD_DIM + 1]
        attended = mixed[:HEAD_DIM] / total
        wide_ref[:, lanes] = attended
        low_ref[:, lanes] = attended.astype(LOW)
        log_ref[0, :, lanes] = peak + jnp.log(total)


def attend_forward(query, keys, values, mask, ones):
    cols, rows = query.shape
    heads = cols // HEAD_DIM
    head = pl.BlockSpec((HEAD_DIM, rows), lambda h: (h, 0))
    shared = pl.BlockSpec((HEAD_DIM, rows), lambda h: (0, 0))
    return pl.pallas_call(
        attend_forward_body,
        grid=(heads,),
        in_specs=[head, head, head, shared, shared],
        out_specs=[head, head, pl.BlockSpec((1, 1, rows), lambda h: (h, 0, 0))],
        out_shape=[
            jax.ShapeDtypeStruct((cols, rows), LOW),
            jax.ShapeDtypeStruct((cols, rows), WIDE),
            jax.ShapeDtypeStruct((heads, 1, rows), WIDE),
        ],
        compiler_params=pltpu.CompilerParams(vmem_limit_bytes=48 * 1024 * 1024),
        cost_estimate=pl.CostEstimate(
            flops=8 * heads * rows * rows * HEAD_DIM,
            bytes_accessed=12 * cols * rows,
            transcendentals=heads * rows * rows,
        ),
    )(query, keys, values, mask, ones)


def attend_backward_body(
    q_ref, k_ref, v_ref, g_ref, wide_ref, log_ref, mask_ref, ones_ref, out_ref
):
    rows = q_ref.shape[1]
    keys_t = k_ref[...]
    keys = with_row(keys_t, mask_ref[...]).T
    query = with_row((q_ref[...].astype(WIDE) * SCALE).astype(LOW), ones_ref[...])
    values = with_row(v_ref[...], mask_ref[...]).T[:, :HEAD_DIM]
    both = with_row(q_ref[...], g_ref[...]).T
    grad_keys = jnp.zeros((rows, HEAD_DIM), WIDE)
    grad_values = jnp.zeros((rows, HEAD_DIM), WIDE)
    for start, size in lane_blocks(rows):
        lanes = slice(start, start + size)
        grad_out = g_ref[:, lanes]
        scores = jnp.dot(keys, query[:, lanes], preferred_element_type=WIDE)
        probs = jnp.exp(scores - log_ref[0, :, lanes])
        grad_probs = jnp.dot(values, grad_out, preferred_element_type=WIDE)
        along = jnp.sum(grad_out.astype(WIDE) * wide_ref[:, lanes], axis=0, keepdims=True)
        grad_scores = (probs * (grad_probs - along)).astype(LOW)
        grad_query = jnp.dot(keys_t, grad_scores, preferred_element_type=WIDE) * SCALE
        out_ref[0, :, lanes] = grad_query.astype(LOW)
        grad_keys += jnp.dot(
            grad_scores, both[lanes, :HEAD_DIM], preferred_element_type=WIDE
        )
        grad_values += jnp.dot(
            probs.astype(LOW), both[lanes, HEAD_DIM:], preferred_element_type=WIDE
        )
    joined = jnp.concatenate((grad_keys * SCALE, grad_values), axis=1).T
    out_ref[1] = joined[:HEAD_DIM].astype(LOW)
    out_ref[2] = joined[HEAD_DIM:].astype(LOW)


def attend_backward(query, keys, values, grad_out, wide, log_total, mask, ones):
    cols, rows = query.shape
    heads = cols // HEAD_DIM
    head = pl.BlockSpec((HEAD_DIM, rows), lambda h: (h, 0))
    shared = pl.BlockSpec((HEAD_DIM, rows), lambda h: (0, 0))
    return pl.pallas_call(
        attend_backward_body,
        grid=(heads,),
        in_specs=[
            head,
            head,
            head,
            head,
            head,
            pl.BlockSpec((1, 1, rows), lambda h: (h, 0, 0)),
            shared,
            shared,
        ],
        out_specs=pl.BlockSpec((3, HEAD_DIM, rows), lambda h: (0, h, 0)),
        out_shape=jax.ShapeDtypeStruct((3, cols, rows), LOW),
        compiler_params=pltpu.CompilerParams(vmem_limit_bytes=48 * 1024 * 1024),
        cost_estimate=pl.CostEstimate(
            flops=16 * heads * rows * rows * HEAD_DIM,
            bytes_accessed=20 * cols * rows,
            transcendentals=heads * rows * rows,
        ),
    )(query, keys, values, grad_out, wide, log_total, mask, ones)


def hidden_body(
    second_ref, grad_ref, expand_ref, shrink_ref, bias_ref,
    hidden_ref, pre_ref, down_ref, back_ref, sum_ref,
):
    preact = jnp.dot(second_ref[...], expand_ref[...], preferred_element_type=WIDE) + bias_ref[...]
    share = 0.5 * (1.0 + lax.erf(preact * 0.5**0.5))
    hidden = (preact * share).astype(LOW)
    slope = share + preact * (jnp.exp(preact * preact * -0.5) * (0.5 / math.pi) ** 0.5)
    grad_hidden = jnp.dot(grad_ref[...], shrink_ref[...], preferred_element_type=WIDE)
    grad_pre = (grad_hidden * slope).astype(LOW)
    hidden_ref[...] = hidden
    pre_ref[...] = grad_pre
    back_ref[...] = times_t(grad_pre, expand_ref[...])
    down_ref[...] = times_t(hidden, shrink_ref[...])
    sums = jnp.sum(grad_pre.astype(WIDE), axis=0, keepdims=True)

    @pl.when(pl.program_id(0) == 0)
    def _():
        sum_ref[...] = sums

    @pl.when(pl.program_id(0) != 0)
    def _():
        sum_ref[...] += sums


def hidden_layer(second, grad, expand, shrink, bias):
    rows, width = second.shape
    cols = expand.shape[1]
    step = rows // 4
    narrow = pl.BlockSpec((step, width), lambda r: (r, 0))
    units = pl.BlockSpec((step, cols), lambda r: (r, 0))
    weight = pl.BlockSpec((width, cols), lambda r: (0, 0))
    line = pl.BlockSpec((1, cols), lambda r: (0, 0))
    return pl.pallas_call(
        hidden_body,
        grid=(4,),
        in_specs=[narrow, narrow, weight, weight, line],
        out_specs=[units, units, narrow, narrow, line],
        out_shape=[
            jax.ShapeDtypeStruct((rows, cols), LOW),
            jax.ShapeDtypeStruct((rows, cols), LOW),
            jax.ShapeDtypeStruct((rows, width), WIDE),
            jax.ShapeDtypeStruct((rows, width), WIDE),
            jax.ShapeDtypeStruct((1, cols), WIDE),
        ],
        compiler_params=pltpu.CompilerParams(vmem_limit_bytes=48 * 1024 * 1024),
        cost_estimate=pl.CostEstimate(
            flops=8 * rows * cols * width,
            bytes_accessed=4 * rows * width + 4 * rows * cols + 8 * rows * width + 4 * width * cols,
            transcendentals=2 * rows * cols,
        ),
    )(second, grad, expand, shrink, bias)


def gather_small(values):
    bit = 1
    place = lax.axis_index("gy")
    while bit < lax.axis_size("gy"):
        other = swap(values, "gy", bit)
        values = jnp.where(
            (place & bit) != 0,
            jnp.concatenate((other, values), axis=0),
            jnp.concatenate((values, other), axis=0),
        )
        bit *= 2
    return values


def token_sums(vectors):
    flat = vectors.reshape(vectors.shape[0], lax.axis_size("gy"), -1)
    flat = flat.transpose(1, 0, 2)
    bit = lax.axis_size("gy") // 2
    place = lax.axis_index("gy")
    while bit:
        half = flat.shape[0] // 2
        upper = (place & bit) != 0
        kept = jnp.where(upper, flat[half:], flat[:half])
        sent = jnp.where(upper, flat[:half], flat[half:])
        flat = kept + swap(sent, "gy", bit)
        bit //= 2
    flat = flat[0]
    bit = 1
    while bit < lax.axis_size("gx"):
        flat = flat + swap(flat, "gx", bit)
        bit *= 2
    return flat


def image_sums(vector):
    bit = 1
    while bit < lax.axis_size("gy"):
        vector = vector + swap(vector, "gy", bit)
        bit *= 2
    return vector


def on_device(
    tokens,
    project_in,
    query_bias,
    value_bias,
    project_out,
    output_bias,
    attention_scale,
    first_norm_gain,
    first_norm_bias,
    second_norm_gain,
    second_norm_bias,
    expand_weight,
    expand_bias,
    shrink_weight,
    shrink_bias,
    feedforward_scale,
    cotangent,
):
    nx, ny = lax.axis_size("gx"), lax.axis_size("gy")
    head_cols = project_out.shape[0]
    hidden_cols = expand_weight.shape[1]
    packed_shape = tokens.shape
    block = -(-SEQ // (nx * 16)) * 16
    column = jnp.arange(block)
    mask = jnp.concatenate(
        [
            jnp.where((lax.axis_index("gx") ^ k) * block + column < SEQ, 0.0, -1e30)
            for k in slot_blocks(nx)
        ]
    )
    top = jnp.arange(HEAD_DIM)[:, None] == 0
    mask = jnp.where(top, mask[None], 0.0).astype(LOW)
    ones = jnp.where(top, jnp.ones((1, nx * block), WIDE), 0.0).astype(LOW)

    small = jnp.stack(
        (
            output_bias,
            attention_scale,
            first_norm_gain,
            first_norm_bias,
            second_norm_gain,
            second_norm_bias,
            shrink_bias,
            feedforward_scale,
        )
    )
    small = gather_small(small[None])
    out_shift, attn_scale, gain_one, shift_one, gain_two, shift_two, shrink_shift, ff_scale = [
        small[:, k].reshape(D) for k in range(8)
    ]
    weights = jnp.concatenate(
        (project_in.reshape(-1, 3 * head_cols), project_out.T, expand_weight, shrink_weight.T),
        axis=1,
    )
    weights = lax.all_gather(weights, "gy", axis=0, tiled=True)
    weight_in, weight_out, weight_expand, weight_shrink = jnp.split(
        weights, (3 * head_cols, 4 * head_cols, 4 * head_cols + hidden_cols), axis=1
    )
    inputs = to_owner(cut_rows(tokens, block)).astype(WIDE)
    grad_parts = cut_rows(cotangent, block)
    inputs, grad_parts = lax.optimization_barrier((inputs, grad_parts))
    grad = to_owner(grad_parts).astype(WIDE)

    first, first_hat, first_rstd = norm_forward(inputs, gain_one, shift_one)
    first_all = gather_rows(first)
    mixed = lax.dot_general(
        weight_in, first_all, (((0,), (1,)), ((), ())), preferred_element_type=WIDE
    )
    query = (mixed[:head_cols] + query_bias[:, None]).astype(LOW)
    keys = mixed[head_cols : 2 * head_cols].astype(LOW)
    values = (mixed[2 * head_cols :] + value_bias[:, None]).astype(LOW)
    attended, attended_wide, log_total = attend_forward(query, keys, values, mask, ones)

    grad_b = grad * ff_scale
    grad_b_all = gather_rows(grad_b.astype(LOW))

    branch_a = scatter_rows(inner_rows(attended, weight_out.T)) + out_shift
    middle = inputs + attn_scale * branch_a
    second, second_hat, second_rstd = norm_forward(middle, gain_two, shift_two)
    second_all = gather_rows(second)
    hidden, grad_pre, branch_part, second_part, pre_sum = hidden_layer(
        second_all, grad_b_all, weight_expand, weight_shrink, expand_bias[None]
    )
    grad_second = scatter_rows(second_part)
    branch_b = scatter_rows(branch_part) + shrink_shift
    output_parts = leave_owner((middle + ff_scale * branch_b).astype(LOW))

    shrink_grad = inner_rows(grad_b_all, hidden)
    expand_grad = inner_rows(second_all, grad_pre)
    wide_grads = jnp.concatenate((shrink_grad, expand_grad), axis=1).astype(LOW)
    wide_grads = lax.psum_scatter(wide_grads, "gy", scatter_dimension=0, tiled=True).astype(WIDE)

    grad_middle = grad + norm_backward(grad_second, gain_two, second_hat, second_rstd)
    grad_a = grad_middle * attn_scale
    grad_a_all = gather_rows(grad_a.astype(LOW))
    grad_attended = lax.dot_general(
        weight_out, grad_a_all, (((0,), (1,)), ((), ())), preferred_element_type=WIDE
    ).astype(LOW)
    grad_mixed = attend_backward(
        query, keys, values, grad_attended, attended_wide, log_total, mask, ones
    )
    block_output = join_rows(output_parts, packed_shape)
    grad_mixed, block_output = lax.optimization_barrier((grad_mixed, block_output))
    joined = grad_mixed.reshape(3 * head_cols, nx * block)
    grad_first = scatter_rows(inner_rows(joined, weight_in.T))
    input_gradient = grad_middle + norm_backward(grad_first, gain_one, first_hat, first_rstd)
    input_gradient = join_rows(leave_owner(input_gradient.astype(LOW)), packed_shape).astype(WIDE)

    out_grad = times_t(attended, grad_a_all.T).T
    in_grad = times_t(joined, first_all.T).T
    head_grads = jnp.concatenate((out_grad, in_grad), axis=1).astype(LOW)
    head_grads = lax.psum_scatter(head_grads, "gy", scatter_dimension=0, tiled=True).astype(WIDE)

    sums = token_sums(
        jnp.stack(
            [
                jnp.sum(item, axis=0)
                for item in (
                    grad_a,
                    grad_middle * branch_a,
                    grad_first * first_hat,
                    grad_first,
                    grad_second * second_hat,
                    grad_second,
                    grad_b,
                    grad * branch_b,
                )
            ]
        )
    )
    biases = image_sums(
        jnp.concatenate(
            (
                jnp.sum(grad_mixed[0].astype(WIDE), axis=1),
                jnp.sum(grad_mixed[2].astype(WIDE), axis=1),
                pre_sum[0],
            )
        )
    )
    return (
        block_output,
        input_gradient,
        head_grads[:, head_cols:].reshape(-1, 3, head_cols),
        biases[:head_cols],
        biases[head_cols : 2 * head_cols],
        head_grads[:, :head_cols].T,
        sums[0],
        sums[1],
        sums[2],
        sums[3],
        sums[4],
        sums[5],
        wide_grads[:, hidden_cols:],
        biases[2 * head_cols :],
        wide_grads[:, :hidden_cols].T,
        sums[6],
        sums[7],
    )


def solution(mesh):
    rows = P("gx", "gy", None)
    wide, heads = P("gy"), P("gx")
    placed = (
        rows, P("gy", None, "gx"), heads, heads, P("gx", "gy"), wide, wide, wide, wide, wide, wide,
        P("gy", "gx"), heads, P("gx", "gy"), wide, wide, rows,
    )
    results = (
        rows, rows, P("gy", None, "gx"), heads, heads, P("gx", "gy"), wide, wide, wide, wide, wide,
        wide, P("gy", "gx"), heads, P("gx", "gy"), wide, wide,
    )
    return jax.shard_map(
        on_device, mesh=mesh, in_specs=placed, out_specs=results, check_vma=False
    )
```

```python
import math

import jax
import jax.numpy as jnp
from jax import lax
from jax.experimental import pallas as pl
from jax.experimental.pallas import tpu as pltpu
from jax.sharding import PartitionSpec as P

D = 1024
HEAD_DIM = 64
SEQ = 1370
SCALE = HEAD_DIM ** (-0.5)
LOW = jnp.bfloat16
WIDE = jnp.float32


def swap(values, axis, bit):
    size = lax.axis_size(axis)
    return lax.ppermute(values, axis, [(k, k ^ bit) for k in range(size)])


def together(*values):
    return lax.optimization_barrier(values)


def gather_far(values):
    bit = lax.axis_size("gx") // 2
    while bit > 2:
        values = jnp.concatenate((values, swap(values, "gx", bit)), axis=0)
        bit //= 2
    return values, swap(values, "gx", 2)


def gather_step(values):
    return jnp.concatenate(gather_far(values), axis=0)


def gather_halves(values):
    near = gather_step(values)
    return near, swap(near, "gx", 1)


def slot_blocks(count):
    order = [0]
    bit = count // 2
    while bit:
        order = order + [k ^ bit for k in order]
        bit //= 2
    return order


def scatter_near(kept, sent):
    return kept + swap(sent, "gx", 1).astype(WIDE)


def scatter_last(partial):
    bit = 2
    while True:
        half = partial.shape[0] // 2
        received = swap(partial[half:].astype(LOW), "gx", bit)
        partial = partial[:half]
        bit *= 2
        if bit >= lax.axis_size("gx"):
            return partial, received
        partial = partial + received.astype(WIDE)


def scatter_far(partial):
    kept, received = scatter_last(partial)
    return kept + received.astype(WIDE)


def in_two(partial):
    half = partial.shape[0] // 2
    return partial[:half], partial[half:].astype(LOW)


def pieces(values, count):
    parts = []
    for _ in range(count):
        head = lax.reduce_precision(values, exponent_bits=8, mantissa_bits=7)
        parts.append(head.astype(LOW))
        values = values - head
    return parts


def reversed_bits(value, count):
    turned = 0
    while count > 1:
        turned = turned * 2 + value % 2
        value //= 2
        count //= 2
    return turned


def owner_pairs(nx, ny):
    return [
        (i * ny + h * nx + q, reversed_bits(q, nx) * ny + h * nx + reversed_bits(i, nx))
        for i in range(nx)
        for h in range(ny // nx)
        for q in range(nx)
    ]


def cut_rows(values, block):
    nx, ny = lax.axis_size("gx"), lax.axis_size("gy")
    images = values.reshape(ny // nx, SEQ, D // ny)
    images = jnp.pad(images, ((0, 0), (0, nx * block - SEQ), (0, 0)))
    parts = images.reshape(ny // nx, nx, block, D // ny)
    parts = jnp.stack([parts[:, reversed_bits(q, nx)] for q in range(nx)], axis=1)
    return parts.reshape(ny, block, D // ny)


def cross(parts, extra=None):
    if extra is None:
        return lax.all_to_all(parts, "gy", split_axis=0, concat_axis=0, tiled=True), None
    rows, more = parts.shape[1], extra.shape[1]
    parts = jnp.concatenate((parts, jnp.pad(extra, ((0, 0), (0, -more % 16), (0, 0)))), axis=1)
    parts = lax.all_to_all(parts, "gy", split_axis=0, concat_axis=0, tiled=True)
    return parts[:, :rows], parts[:, rows : rows + more]


def spread_lines(values):
    ny = lax.axis_size("gy")
    lines = jnp.concatenate([item.reshape(-1, D // ny) for item in pieces(values, 2)], axis=0)
    return jnp.broadcast_to(lines[None], (ny,) + lines.shape)


def split_lines(vectors):
    ny = lax.axis_size("gy")
    lines = jnp.concatenate(pieces(vectors, 2), axis=0)
    return lines.reshape(-1, ny, D // ny).transpose(1, 0, 2)


def sum_lines(lines):
    return jnp.sum(lines.astype(WIDE), axis=0).reshape(2, -1, lines.shape[2]).sum(axis=0)


def move_to_owner(parts):
    nx, ny = lax.axis_size("gx"), lax.axis_size("gy")
    return lax.ppermute(parts, ("gx", "gy"), owner_pairs(nx, ny))


def join_width(parts):
    return parts.transpose(1, 0, 2).reshape(parts.shape[1], D)


def to_owner(parts):
    return join_width(move_to_owner(parts))


def leave_owner(values):
    nx, ny = lax.axis_size("gx"), lax.axis_size("gy")
    parts = values.reshape(values.shape[0], ny, D // ny).transpose(1, 0, 2)
    return lax.ppermute(parts, ("gx", "gy"), [(b, a) for a, b in owner_pairs(nx, ny)])


def join_rows(parts, packed_shape):
    nx, ny = lax.axis_size("gx"), lax.axis_size("gy")
    block = parts.shape[1]
    parts = parts.reshape(ny // nx, nx, block, D // ny)
    parts = jnp.stack([parts[:, reversed_bits(q, nx)] for q in range(nx)], axis=1)
    return parts.reshape(ny // nx, nx * block, D // ny)[:, :SEQ].reshape(packed_shape)


def norm_forward(values, gain, shift):
    center = jnp.mean(values, axis=1, keepdims=True)
    spread = jnp.mean(values * values, axis=1, keepdims=True) - center * center
    rstd = lax.rsqrt(spread + 1e-06)
    normed = (values - center) * rstd
    return (normed * gain + shift).astype(LOW), normed, rstd


def norm_backward(grad, gain, normed, rstd):
    scaled = grad * gain
    total = jnp.mean(scaled, axis=1, keepdims=True)
    along = jnp.mean(scaled * normed, axis=1, keepdims=True)
    return rstd * (scaled - total - normed * along)


def times(left, right):
    return jnp.dot(left, right, preferred_element_type=WIDE)


def times_t(left, right):
    return lax.dot_general(left, right, (((1,), (1,)), ((), ())), preferred_element_type=WIDE)


def inner_rows(left, right):
    return lax.dot_general(left, right, (((0,), (0,)), ((), ())), preferred_element_type=WIDE)


def lane_blocks(size):
    return [(start, min(256, size - start)) for start in range(0, size, 256)]


def with_row(head, row):
    return jnp.concatenate((head, row), axis=0)


def attend_forward_body(q_ref, k_ref, v_ref, mask_ref, ones_ref, *refs):
    low_ref, wide_ref, log_ref = refs[-3:]
    keys = with_row(k_ref[...], mask_ref[...]).T
    query = with_row((q_ref[...].astype(WIDE) * SCALE).astype(LOW), ones_ref[...])
    values = with_row(v_ref[...], ones_ref[...])
    for start, size in lane_blocks(query.shape[1]):
        lanes = slice(start, start + size)
        scores = jnp.dot(keys, query[:, lanes], preferred_element_type=WIDE)
        peak = jnp.max(scores, axis=0, keepdims=True)
        raised = jnp.exp(scores - peak).astype(LOW)
        mixed = jnp.dot(values, raised, preferred_element_type=WIDE)
        total = mixed[HEAD_DIM : HEAD_DIM + 1]
        attended = mixed[:HEAD_DIM] / total
        wide_ref[:, lanes] = attended
        low_ref[:, lanes] = attended.astype(LOW)
        log_ref[0, :, lanes] = peak + jnp.log(total)


def attend_forward(query, keys, values, mask, ones, first_head, count, before=()):
    cols, rows = query.shape
    heads = cols // HEAD_DIM
    head = pl.BlockSpec((HEAD_DIM, rows), lambda h: (h + first_head, 0))
    shared = pl.BlockSpec((HEAD_DIM, rows), lambda h: (0, 0))
    return pl.pallas_call(
        attend_forward_body,
        grid=(count,),
        in_specs=[head, head, head, shared, shared] + [pl.BlockSpec(memory_space=pl.ANY)] * len(before),
        out_specs=[head, head, pl.BlockSpec((1, 1, rows), lambda h: (h + first_head, 0, 0))],
        out_shape=[
            jax.ShapeDtypeStruct((cols, rows), LOW),
            jax.ShapeDtypeStruct((cols, rows), WIDE),
            jax.ShapeDtypeStruct((heads, 1, rows), WIDE),
        ],
        input_output_aliases={5 + k: k for k in range(len(before))},
        compiler_params=pltpu.CompilerParams(vmem_limit_bytes=40 * 1024 * 1024),
        cost_estimate=pl.CostEstimate(
            flops=48 * count * rows * rows * HEAD_DIM,
            bytes_accessed=12 * count * HEAD_DIM * rows,
            transcendentals=count * rows * rows,
        ),
    )(query, keys, values, mask, ones, *before)


def attend_backward_body(
    q_ref, k_ref, v_ref, g_ref, wide_ref, log_ref, mask_ref, ones_ref, *refs
):
    out_ref = refs[-1]
    rows = q_ref.shape[1]
    keys_t = k_ref[...]
    keys = with_row(keys_t, mask_ref[...]).T
    query = with_row((q_ref[...].astype(WIDE) * SCALE).astype(LOW), ones_ref[...])
    values = with_row(v_ref[...], mask_ref[...]).T[:, :HEAD_DIM]
    both = with_row(q_ref[...], g_ref[...]).T
    grad_keys = jnp.zeros((rows, HEAD_DIM), WIDE)
    grad_values = jnp.zeros((rows, HEAD_DIM), WIDE)
    for start, size in lane_blocks(rows):
        lanes = slice(start, start + size)
        grad_out = g_ref[:, lanes]
        scores = jnp.dot(keys, query[:, lanes], preferred_element_type=WIDE)
        probs = jnp.exp(scores - log_ref[0, :, lanes])
        grad_probs = jnp.dot(values, grad_out, preferred_element_type=WIDE)
        along = jnp.sum(grad_out.astype(WIDE) * wide_ref[:, lanes], axis=0, keepdims=True)
        grad_scores = (probs * (grad_probs - along)).astype(LOW)
        grad_query = jnp.dot(keys_t, grad_scores, preferred_element_type=WIDE) * SCALE
        out_ref[0, :, lanes] = grad_query.astype(LOW)
        grad_keys += jnp.dot(
            grad_scores, both[lanes, :HEAD_DIM], preferred_element_type=WIDE
        )
        grad_values += jnp.dot(
            probs.astype(LOW), both[lanes, HEAD_DIM:], preferred_element_type=WIDE
        )
    joined = jnp.concatenate((grad_keys * SCALE, grad_values), axis=1).T
    out_ref[1] = joined[:HEAD_DIM].astype(LOW)
    out_ref[2] = joined[HEAD_DIM:].astype(LOW)


def attend_backward(
    query, keys, values, grad_out, wide, log_total, mask, ones, first_head, count, before=()
):
    cols, rows = query.shape
    head = pl.BlockSpec((HEAD_DIM, rows), lambda h: (h + first_head, 0))
    shared = pl.BlockSpec((HEAD_DIM, rows), lambda h: (0, 0))
    return pl.pallas_call(
        attend_backward_body,
        grid=(count,),
        in_specs=[
            head,
            head,
            head,
            head,
            head,
            pl.BlockSpec((1, 1, rows), lambda h: (h + first_head, 0, 0)),
            shared,
            shared,
        ]
        + [pl.BlockSpec(memory_space=pl.ANY)] * len(before),
        out_specs=pl.BlockSpec((3, HEAD_DIM, rows), lambda h: (0, h + first_head, 0)),
        out_shape=jax.ShapeDtypeStruct((3, cols, rows), LOW),
        input_output_aliases={8 + k: k for k in range(len(before))},
        compiler_params=pltpu.CompilerParams(vmem_limit_bytes=40 * 1024 * 1024),
        cost_estimate=pl.CostEstimate(
            flops=56 * count * rows * rows * HEAD_DIM,
            bytes_accessed=20 * count * HEAD_DIM * rows,
            transcendentals=count * rows * rows,
        ),
    )(query, keys, values, grad_out, wide, log_total, mask, ones, *before)


def forward_body(
    near_ref, far_ref, expand_ref, shrink_ref, bias_ref, hidden_ref, slope_ref, kept_ref, sent_ref
):
    def work(rows_ref, down_ref):
        preact = jnp.dot(rows_ref[...], expand_ref[...], preferred_element_type=WIDE)
        preact = preact + bias_ref[...]
        share = 0.5 * (1.0 + lax.erf(preact * 0.5**0.5))
        hidden = (preact * share).astype(LOW)
        hidden_ref[...] = hidden
        bell = jnp.exp(preact * preact * -0.5) * (0.5 / math.pi) ** 0.5
        slope_ref[...] = share + preact * bell
        down_ref[...] = times_t(hidden, shrink_ref[...]).astype(down_ref.dtype)

    @pl.when(pl.program_id(0) < 2)
    def _():
        work(far_ref, sent_ref)

    @pl.when(pl.program_id(0) >= 2)
    def _():
        work(near_ref, kept_ref)


def backward_body(
    near_ref, far_ref, expand_ref, shrink_ref, slope_ref, pre_ref, kept_ref, sent_ref, sum_ref
):
    def work(rows_ref, back_ref):
        grad_hidden = jnp.dot(rows_ref[...], shrink_ref[...], preferred_element_type=WIDE)
        grad_pre = (grad_hidden * slope_ref[...]).astype(LOW)
        pre_ref[...] = grad_pre
        back_ref[...] = times_t(grad_pre, expand_ref[...]).astype(back_ref.dtype)
        sums = jnp.sum(grad_pre.astype(WIDE), axis=0, keepdims=True)

        @pl.when(pl.program_id(0) == 0)
        def _():
            sum_ref[...] = sums

        @pl.when(pl.program_id(0) != 0)
        def _():
            sum_ref[...] += sums

    @pl.when(pl.program_id(0) < 2)
    def _():
        work(far_ref, sent_ref)

    @pl.when(pl.program_id(0) >= 2)
    def _():
        work(near_ref, kept_ref)


def hidden_specs(rows, width, cols):
    step = rows // 2
    near = pl.BlockSpec((step, width), lambda r: (jnp.maximum(r - 2, 0), 0))
    far = pl.BlockSpec((step, width), lambda r: (jnp.minimum(r, 1), 0))
    units = pl.BlockSpec((step, cols), lambda r: ((r + 2) % 4, 0))
    weight = pl.BlockSpec((width, cols), lambda r: (0, 0))
    line = pl.BlockSpec((1, cols), lambda r: (0, 0))
    return near, far, units, weight, line


def hidden_cost(rows, width, cols):
    return pl.CostEstimate(
        flops=16 * rows * cols * width,
        bytes_accessed=10 * rows * width + 12 * rows * cols + 4 * width * cols,
        transcendentals=4 * rows * cols,
    )


def hidden_forward(near_rows, far_rows, expand, shrink, bias):
    rows, width = near_rows.shape
    cols = expand.shape[1]
    near, far, units, weight, line = hidden_specs(rows, width, cols)
    return pl.pallas_call(
        forward_body,
        grid=(4,),
        in_specs=[near, far, weight, weight, line],
        out_specs=[units, units, near, far],
        out_shape=[
            jax.ShapeDtypeStruct((2 * rows, cols), LOW),
            jax.ShapeDtypeStruct((2 * rows, cols), WIDE),
            jax.ShapeDtypeStruct((rows, width), WIDE),
            jax.ShapeDtypeStruct((rows, width), LOW),
        ],
        compiler_params=pltpu.CompilerParams(vmem_limit_bytes=40 * 1024 * 1024),
        cost_estimate=hidden_cost(rows, width, cols),
    )(near_rows, far_rows, expand, shrink, bias)


def hidden_backward(near_rows, far_rows, expand, shrink, slope):
    rows, width = near_rows.shape
    cols = expand.shape[1]
    near, far, units, weight, line = hidden_specs(rows, width, cols)
    return pl.pallas_call(
        backward_body,
        grid=(4,),
        in_specs=[near, far, weight, weight, units],
        out_specs=[units, near, far, line],
        out_shape=[
            jax.ShapeDtypeStruct((2 * rows, cols), LOW),
            jax.ShapeDtypeStruct((rows, width), WIDE),
            jax.ShapeDtypeStruct((rows, width), LOW),
            jax.ShapeDtypeStruct((1, cols), WIDE),
        ],
        compiler_params=pltpu.CompilerParams(vmem_limit_bytes=40 * 1024 * 1024),
        cost_estimate=hidden_cost(rows, width, cols),
    )(near_rows, far_rows, expand, shrink, slope)


def unit_grads_body(
    gn_ref, gf_ref, sn_ref, sf_ref, hidden_ref, pre_ref, out_ref
):
    half = gn_ref.shape[0]

    def work(near_ref, far_ref, units_ref):
        total = inner_rows(near_ref[...], units_ref[:half])
        total += inner_rows(far_ref[...], units_ref[half:])
        out_ref[...] = total.astype(LOW)

    @pl.when(pl.program_id(0) < 4)
    def _():
        work(gn_ref, gf_ref, hidden_ref)

    @pl.when(pl.program_id(0) >= 4)
    def _():
        work(sn_ref, sf_ref, pre_ref)


def unit_grads(grad_near, grad_far, second_near, second_far, hidden, grad_pre):
    half, width = grad_near.shape
    rows, cols = hidden.shape
    tile = width // 4
    early = pl.BlockSpec((half, tile), lambda r: (0, jnp.minimum(r, 3)))
    late = pl.BlockSpec((half, tile), lambda r: (0, jnp.maximum(r - 4, 0)))
    whole = pl.BlockSpec((rows, cols), lambda r: (0, 0))
    return pl.pallas_call(
        unit_grads_body,
        grid=(8,),
        in_specs=[early, early, late, late, whole, whole],
        out_specs=pl.BlockSpec((tile, cols), lambda r: (r % 4, r // 4)),
        out_shape=jax.ShapeDtypeStruct((width, 2 * cols), LOW),
        compiler_params=pltpu.CompilerParams(vmem_limit_bytes=40 * 1024 * 1024),
        cost_estimate=pl.CostEstimate(
            flops=8 * rows * cols * width,
            bytes_accessed=4 * rows * (width + cols) + 4 * width * cols,
            transcendentals=0,
        ),
    )(grad_near, grad_far, second_near, second_far, hidden, grad_pre)


def head_grads_body(place_ref, first_ref, grad_ref, mixed_ref, attended_ref, kept_ref, sent_ref):
    cols = mixed_ref.shape[0]
    heads = times(mixed_ref[...], first_ref[...]).T
    tail = times(attended_ref[...], grad_ref[...]).T
    half = pl.num_programs(0) // 2

    @pl.when(pl.program_id(0) < half)
    def _():
        sent_ref[:, :cols] = heads.astype(LOW)
        sent_ref[:, cols:] = tail.astype(LOW)

    @pl.when(pl.program_id(0) >= half)
    def _():
        kept_ref[:, :cols] = heads
        kept_ref[:, cols:] = tail


def head_grads_of(first, grad, mixed, attended):
    rows, width = first.shape
    cols, more = mixed.shape[0], attended.shape[0]
    tile = 128
    tiles = width // tile
    bits = tiles.bit_length() - 1

    def block(r, place):
        slot = (r + tiles // 2) % tiles
        turned = slot * 0
        for k in range(bits):
            turned = turned * 2 + (slot // 2**k) % 2
        return turned ^ place[0]

    narrow = pl.BlockSpec((rows, tile), lambda r, place: (0, block(r, place)))
    return pl.pallas_call(
        head_grads_body,
        grid_spec=pltpu.PrefetchScalarGridSpec(
            num_scalar_prefetch=1,
            grid=(tiles,),
            in_specs=[
                narrow,
                narrow,
                pl.BlockSpec((cols, rows), lambda r, place: (0, 0)),
                pl.BlockSpec((more, rows), lambda r, place: (0, 0)),
            ],
            out_specs=[
                pl.BlockSpec(
                    (tile, cols + more), lambda r, place: (jnp.maximum(r - tiles // 2, 0), 0)
                ),
                pl.BlockSpec(
                    (tile, cols + more), lambda r, place: (jnp.minimum(r, tiles // 2 - 1), 0)
                ),
            ],
        ),
        out_shape=[
            jax.ShapeDtypeStruct((width // 2, cols + more), WIDE),
            jax.ShapeDtypeStruct((width // 2, cols + more), LOW),
        ],
        compiler_params=pltpu.CompilerParams(vmem_limit_bytes=40 * 1024 * 1024),
        cost_estimate=pl.CostEstimate(
            flops=4 * rows * (cols + more) * width,
            bytes_accessed=2 * rows * (2 * width + cols + more) + 3 * width * (cols + more),
            transcendentals=0,
        ),
    )(lax.axis_index("gy").astype(jnp.int32)[None], first, grad, mixed, attended)


def plain_head_grads(first, grad, mixed, attended):
    joined = jnp.concatenate((times(mixed, first).T, times(attended, grad).T), axis=1).astype(LOW)
    return lax.psum_scatter(joined, "gy", scatter_dimension=0, tiled=True).astype(WIDE)


def scatter_head_grads(first, grad, mixed, attended):
    ny = lax.axis_size("gy")
    if D // ny != 128:
        return plain_head_grads(first, grad, mixed, attended)
    kept, sent = head_grads_of(first, grad, mixed, attended)
    total = kept + swap(sent, "gy", 1).astype(WIDE)
    bit = 2
    while bit < ny:
        half = total.shape[0] // 2
        received = swap(total[half:].astype(LOW), "gy", bit)
        total = total[:half] + received.astype(WIDE)
        bit *= 2
    return total


def on_device(
    tokens,
    project_in,
    query_bias,
    value_bias,
    project_out,
    output_bias,
    attention_scale,
    first_norm_gain,
    first_norm_bias,
    second_norm_gain,
    second_norm_bias,
    expand_weight,
    expand_bias,
    shrink_weight,
    shrink_bias,
    feedforward_scale,
    cotangent,
):
    nx, ny = lax.axis_size("gx"), lax.axis_size("gy")
    head_cols = project_out.shape[0]
    hidden_cols = expand_weight.shape[1]
    packed_shape = tokens.shape
    block = -(-SEQ // (nx * 16)) * 16
    column = jnp.arange(block)
    mask = jnp.concatenate(
        [
            jnp.where((lax.axis_index("gx") ^ k) * block + column < SEQ, 0.0, -1e30)
            for k in slot_blocks(nx)
        ]
    )
    top = jnp.arange(HEAD_DIM)[:, None] == 0
    mask = jnp.where(top, mask[None], 0.0).astype(LOW)
    ones = jnp.where(top, jnp.ones((1, nx * block), WIDE), 0.0).astype(LOW)

    small = jnp.concatenate(
        pieces(
            jnp.stack(
                (
                    output_bias,
                    attention_scale,
                    first_norm_gain,
                    first_norm_bias,
                    second_norm_gain,
                    second_norm_bias,
                    shrink_bias,
                    feedforward_scale,
                )
            ),
            3,
        ),
        axis=0,
    )
    heads_weight = lax.all_gather(
        jnp.concatenate((project_in.reshape(-1, 3 * head_cols), project_out.T), axis=1),
        "gy",
        axis=0,
        tiled=True,
    )
    weight_in, weight_out = heads_weight[:, : 3 * head_cols], heads_weight[:, 3 * head_cols :]
    units_weight = jnp.concatenate((expand_weight, shrink_weight.T), axis=1)

    parts, small = cross(
        jnp.concatenate((cut_rows(tokens, block), cut_rows(cotangent, block)), axis=1),
        jnp.broadcast_to(small[None], (ny,) + small.shape),
    )
    parts, small, units_weight = together(parts, small, units_weight)
    units_weight = lax.all_gather(units_weight, "gy", axis=0, tiled=True)
    weight_expand, weight_shrink = units_weight[:, :hidden_cols], units_weight[:, hidden_cols:]
    small = small.astype(WIDE)
    small = small[:, :8] + (small[:, 8:16] + small[:, 16:])
    out_shift, attn_scale, gain_one, shift_one, gain_two, shift_two, shrink_shift, ff_scale = [
        small[:, k].reshape(D) for k in range(8)
    ]
    inputs = to_owner(parts[:, :block]).astype(WIDE)

    first, first_hat, first_rstd = norm_forward(inputs, gain_one, shift_one)
    first_own, first_far = gather_far(first)
    first_far, grad_parts = together(first_far, parts[:, block:])
    first_near = jnp.concatenate((first_own, first_far), axis=0)
    first_all = jnp.concatenate((first_near, swap(first_near, "gx", 1)), axis=0)
    grad_parts = move_to_owner(grad_parts)
    mixed = lax.dot_general(
        weight_in, first_all, (((0,), (1,)), ((), ())), preferred_element_type=WIDE
    )
    query = (mixed[:head_cols] + query_bias[:, None]).astype(LOW)
    keys = mixed[head_cols : 2 * head_cols].astype(LOW)
    values = (mixed[2 * head_cols :] + value_bias[:, None]).astype(LOW)
    split = head_cols // HEAD_DIM // 2
    half = attend_forward(query, keys, values, mask, ones, 0, split)
    *half, grad_parts = together(*half, grad_parts)
    grad = join_width(grad_parts).astype(WIDE)
    grad_b = grad * ff_scale
    grad_b_own, grad_b_other = gather_far(grad_b.astype(LOW))
    attended, attended_wide, log_total = attend_forward(
        query, keys, values, mask, ones, split, head_cols // HEAD_DIM - split, half
    )
    attended, grad_b_other = together(attended, grad_b_other)
    grad_b_near = jnp.concatenate((grad_b_own, grad_b_other), axis=0)
    grad_b_far = swap(grad_b_near, "gx", 1)

    kept, sent = in_two(inner_rows(attended, weight_out.T))
    branch_a = scatter_far(scatter_near(kept, sent)) + out_shift
    middle = inputs + attn_scale * branch_a
    second, second_hat, second_rstd = norm_forward(middle, gain_two, shift_two)
    second_near, second_far = gather_halves(second)
    hidden, slope, kept_b, sent_b = hidden_forward(
        second_near, second_far, weight_expand, weight_shrink, expand_bias[None]
    )
    branch_near = scatter_near(kept_b, sent_b)
    grad_pre, kept, sent, pre_sum = hidden_backward(
        grad_b_near, grad_b_far, weight_expand, weight_shrink, slope
    )
    wide_grads = unit_grads(grad_b_near, grad_b_far, second_near, second_far, hidden, grad_pre)
    grad_second, wide_grads = together(scatter_far(scatter_near(kept, sent)), wide_grads)
    wide_grads = lax.psum_scatter(wide_grads, "gy", scatter_dimension=0, tiled=True).astype(WIDE)

    grad_middle = grad + norm_backward(grad_second, gain_two, second_hat, second_rstd)
    grad_a = grad_middle * attn_scale
    grad_a_near, branch_near = together(gather_step(grad_a.astype(LOW)), branch_near)
    grad_a_all = jnp.concatenate((grad_a_near, swap(grad_a_near, "gx", 1)), axis=0)
    branch_kept, branch_far = scatter_last(branch_near)
    grad_attended = lax.dot_general(
        weight_out, grad_a_all, (((0,), (1,)), ((), ())), preferred_element_type=WIDE
    ).astype(LOW)
    half = attend_backward(
        query, keys, values, grad_attended, attended_wide, log_total, mask, ones, 0, split
    )
    half, branch_far = together(half, branch_far)
    branch_b = branch_kept + branch_far.astype(WIDE) + shrink_shift
    output_parts = leave_owner((middle + ff_scale * branch_b).astype(LOW))
    grad_mixed = attend_backward(
        query,
        keys,
        values,
        grad_attended,
        attended_wide,
        log_total,
        mask,
        ones,
        split,
        head_cols // HEAD_DIM - split,
        (half,),
    )
    grad_mixed, output_parts = together(grad_mixed, output_parts)
    early = jnp.stack(
        [
            jnp.sum(item, axis=0)
            for item in (grad_second * second_hat, grad_second, grad_b, grad * branch_b)
        ]
    )
    output_parts, lines = cross(
        output_parts, jnp.concatenate((split_lines(early), spread_lines(pre_sum[0])), axis=1)
    )
    block_output = join_rows(output_parts, packed_shape)
    early, pre_sum = sum_lines(lines[:, :8]), sum_lines(lines[:, 8:]).reshape(-1)

    joined = grad_mixed.reshape(3 * head_cols, nx * block)
    kept, sent = in_two(inner_rows(joined, weight_in.T))
    near, joined = together(scatter_near(kept, sent), joined)
    grad_first = scatter_far(near)
    head_grads = scatter_head_grads(first_all, grad_a_all, joined, attended)
    input_gradient = grad_middle + norm_backward(grad_first, gain_one, first_hat, first_rstd)
    input_parts = leave_owner(input_gradient.astype(LOW))
    late = jnp.stack(
        [
            jnp.sum(item, axis=0)
            for item in (grad_a, grad_middle * branch_a, grad_first * first_hat, grad_first)
        ]
    )
    head_sums = jnp.concatenate(
        (
            jnp.sum(grad_mixed[0].astype(WIDE), axis=1),
            jnp.sum(grad_mixed[2].astype(WIDE), axis=1),
        )
    )
    input_parts, lines = cross(
        input_parts, jnp.concatenate((split_lines(late), spread_lines(head_sums)), axis=1)
    )
    input_gradient = join_rows(input_parts, packed_shape).astype(WIDE)
    late, head_sums = sum_lines(lines[:, :8]), sum_lines(lines[:, 8:]).reshape(-1)
    sums = jnp.concatenate((late, early), axis=0)
    bit = 1
    while bit < nx:
        sums = sums + swap(sums, "gx", bit)
        bit *= 2
    return (
        block_output,
        input_gradient,
        head_grads[:, : 3 * head_cols].reshape(-1, 3, head_cols),
        head_sums[:head_cols],
        head_sums[head_cols:],
        head_grads[:, 3 * head_cols :].T,
        sums[0],
        sums[1],
        sums[2],
        sums[3],
        sums[4],
        sums[5],
        wide_grads[:, hidden_cols:],
        pre_sum,
        wide_grads[:, :hidden_cols].T,
        sums[6],
        sums[7],
    )


def solution(mesh):
    rows = P("gx", "gy", None)
    wide, heads = P("gy"), P("gx")
    placed = (
        rows, P("gy", None, "gx"), heads, heads, P("gx", "gy"), wide, wide, wide, wide, wide, wide,
        P("gy", "gx"), heads, P("gx", "gy"), wide, wide, rows,
    )
    results = (
        rows, rows, P("gy", None, "gx"), heads, heads, P("gx", "gy"), wide, wide, wide, wide, wide,
        wide, P("gy", "gx"), heads, P("gx", "gy"), wide, wide,
    )
    return jax.shard_map(
        on_device, mesh=mesh, in_specs=placed, out_specs=results, check_vma=False
    )
```

```python
import math

import jax
import jax.numpy as jnp
from jax import lax
from jax.experimental import pallas as pl
from jax.experimental.pallas import tpu as pltpu
from jax.sharding import PartitionSpec as P

D = 1024
HEAD_DIM = 64
SEQ = 1370
SCALE = HEAD_DIM ** (-0.5)
LOW = jnp.bfloat16
WIDE = jnp.float32


def swap(values, axis, bit):
    size = lax.axis_size(axis)
    return lax.ppermute(values, axis, [(k, k ^ bit) for k in range(size)])


def together(*values):
    return lax.optimization_barrier(values)


def gather_far(values):
    bit = lax.axis_size("gx") // 2
    while bit > 2:
        values = jnp.concatenate((values, swap(values, "gx", bit)), axis=0)
        bit //= 2
    return values, swap(values, "gx", 2)


def gather_step(values):
    return jnp.concatenate(gather_far(values), axis=0)


def gather_halves(values):
    near = gather_step(values)
    return near, swap(near, "gx", 1)


def slot_blocks(count):
    order = [0]
    bit = count // 2
    while bit:
        order = order + [k ^ bit for k in order]
        bit //= 2
    return order


def scatter_near(kept, sent):
    return kept + swap(sent, "gx", 1).astype(WIDE)


def scatter_last(partial):
    bit = 2
    while True:
        half = partial.shape[0] // 2
        received = swap(partial[half:].astype(LOW), "gx", bit)
        partial = partial[:half]
        bit *= 2
        if bit >= lax.axis_size("gx"):
            return partial, received
        partial = partial + received.astype(WIDE)


def scatter_far(partial):
    kept, received = scatter_last(partial)
    return kept + received.astype(WIDE)


def scatter_step(total, bit):
    half = total.shape[0] // 2
    return total[:half], swap(total[half:].astype(LOW), "gy", bit)


def pieces(values, count):
    parts = []
    for _ in range(count):
        head = lax.reduce_precision(values, exponent_bits=8, mantissa_bits=7)
        parts.append(head.astype(LOW))
        values = values - head
    return parts


def spread_images(values, block):
    nx, ny = lax.axis_size("gx"), lax.axis_size("gy")
    images = values.reshape(ny // nx, SEQ, D // ny)
    images = jnp.pad(images, ((0, 0), (0, nx * block - SEQ), (0, 0)))
    return images.reshape(ny // nx, nx, block, D // ny).transpose(1, 0, 2, 3)


def to_rows(parts):
    parts = lax.all_to_all(parts, "gx", split_axis=0, concat_axis=0, tiled=True)
    return parts.reshape((-1,) + parts.shape[2:])


def to_images(parts):
    nx, ny = lax.axis_size("gx"), lax.axis_size("gy")
    parts = parts.reshape((nx, ny // nx) + parts.shape[1:])
    return lax.all_to_all(parts, "gx", split_axis=0, concat_axis=0, tiled=True)


def join_images(parts, packed_shape):
    nx, per, block, width = parts.shape
    parts = parts.transpose(1, 0, 2, 3).reshape(per, nx * block, width)
    return parts[:, :SEQ].reshape(packed_shape)


def over_rows(sums):
    bit = 1
    while bit < lax.axis_size("gx"):
        sums = sums + swap(sums, "gx", bit)
        bit *= 2
    return sums


def cross(parts, *extra):
    if extra:
        rows = sum(item.shape[1] for item in extra)
        space = jnp.zeros((parts.shape[0], -rows % 16, parts.shape[2]), LOW)
        parts = jnp.concatenate((parts, *extra, space), axis=1)
    return lax.all_to_all(parts, "gy", split_axis=0, concat_axis=0, tiled=True)


def spread_lines(values):
    ny = lax.axis_size("gy")
    lines = jnp.concatenate([item.reshape(-1, D // ny) for item in pieces(values, 2)], axis=0)
    return jnp.broadcast_to(lines[None], (ny,) + lines.shape)


def split_lines(vectors):
    ny = lax.axis_size("gy")
    lines = jnp.concatenate(pieces(vectors, 2), axis=0)
    return lines.reshape(-1, ny, D // ny).transpose(1, 0, 2)


def sum_lines(lines):
    return jnp.sum(lines.astype(WIDE), axis=0).reshape(2, -1, lines.shape[2]).sum(axis=0)


def join_width(parts):
    return parts.transpose(1, 0, 2).reshape(parts.shape[1], D)


def cut_width(values):
    ny = lax.axis_size("gy")
    return values.reshape(values.shape[0], ny, D // ny).transpose(1, 0, 2)


def gather_weight(weight):
    place = lax.axis_index("gy")
    rows, cols = weight.shape
    weight = weight[None]
    bit = lax.axis_size("gy") // 2
    while bit:
        other = swap(weight, "gy", bit)
        upper = (place & bit) != 0
        low, high = jnp.where(upper, other, weight), jnp.where(upper, weight, other)
        weight = jnp.stack((low, high), axis=1).reshape(-1, rows, cols)
        bit //= 2
    return weight.reshape(-1, cols)


def norm_forward(values, gain, shift):
    center = jnp.mean(values, axis=1, keepdims=True)
    spread = jnp.mean(values * values, axis=1, keepdims=True) - center * center
    rstd = lax.rsqrt(spread + 1e-06)
    normed = (values - center) * rstd
    return (normed * gain + shift).astype(LOW), normed, rstd


def norm_backward(grad, gain, normed, rstd):
    scaled = grad * gain
    total = jnp.mean(scaled, axis=1, keepdims=True)
    along = jnp.mean(scaled * normed, axis=1, keepdims=True)
    return rstd * (scaled - total - normed * along)


def times(left, right):
    return jnp.dot(left, right, preferred_element_type=WIDE)


def times_t(left, right):
    return lax.dot_general(left, right, (((1,), (1,)), ((), ())), preferred_element_type=WIDE)


def inner_rows(left, right):
    return lax.dot_general(left, right, (((0,), (0,)), ((), ())), preferred_element_type=WIDE)


def lane_blocks(size):
    return [(start, min(256, size - start)) for start in range(0, size, 256)]


def with_row(head, row):
    return jnp.concatenate((head, row), axis=0)


def attend_forward_body(q_ref, k_ref, v_ref, mask_ref, ones_ref, *refs):
    low_ref, wide_ref, log_ref = refs[-3:]
    keys = with_row(k_ref[...], mask_ref[...]).T
    query = with_row((q_ref[...].astype(WIDE) * SCALE).astype(LOW), ones_ref[...])
    values = with_row(v_ref[...], ones_ref[...])
    for start, size in lane_blocks(query.shape[1]):
        lanes = slice(start, start + size)
        scores = jnp.dot(keys, query[:, lanes], preferred_element_type=WIDE)
        peak = jnp.max(scores, axis=0, keepdims=True)
        raised = jnp.exp(scores - peak).astype(LOW)
        mixed = jnp.dot(values, raised, preferred_element_type=WIDE)
        total = mixed[HEAD_DIM : HEAD_DIM + 1]
        attended = mixed[:HEAD_DIM] / total
        wide_ref[:, lanes] = attended
        low_ref[:, lanes] = attended.astype(LOW)
        log_ref[0, :, lanes] = peak + jnp.log(total)


def attend_forward(query, keys, values, mask, ones, first_head, count, before=()):
    cols, rows = query.shape
    heads = cols // HEAD_DIM
    head = pl.BlockSpec((HEAD_DIM, rows), lambda h: (h + first_head, 0))
    shared = pl.BlockSpec((HEAD_DIM, rows), lambda h: (0, 0))
    return pl.pallas_call(
        attend_forward_body,
        grid=(count,),
        in_specs=[head, head, head, shared, shared] + [pl.BlockSpec(memory_space=pl.ANY)] * len(before),
        out_specs=[head, head, pl.BlockSpec((1, 1, rows), lambda h: (h + first_head, 0, 0))],
        out_shape=[
            jax.ShapeDtypeStruct((cols, rows), LOW),
            jax.ShapeDtypeStruct((cols, rows), WIDE),
            jax.ShapeDtypeStruct((heads, 1, rows), WIDE),
        ],
        input_output_aliases={5 + k: k for k in range(len(before))},
        compiler_params=pltpu.CompilerParams(vmem_limit_bytes=40 * 1024 * 1024),
        cost_estimate=pl.CostEstimate(
            flops=48 * count * rows * rows * HEAD_DIM,
            bytes_accessed=12 * count * HEAD_DIM * rows,
            transcendentals=count * rows * rows,
        ),
    )(query, keys, values, mask, ones, *before)


def attend_backward_body(
    q_ref, k_ref, v_ref, g_ref, wide_ref, log_ref, mask_ref, ones_ref, *refs
):
    out_ref = refs[-1]
    rows = q_ref.shape[1]
    keys_t = k_ref[...]
    keys = with_row(keys_t, mask_ref[...]).T
    query = with_row((q_ref[...].astype(WIDE) * SCALE).astype(LOW), ones_ref[...])
    values = with_row(v_ref[...], mask_ref[...]).T[:, :HEAD_DIM]
    both = with_row(q_ref[...], g_ref[...]).T
    grad_keys = jnp.zeros((rows, HEAD_DIM), WIDE)
    grad_values = jnp.zeros((rows, HEAD_DIM), WIDE)
    for start, size in lane_blocks(rows):
        lanes = slice(start, start + size)
        grad_out = g_ref[:, lanes]
        scores = jnp.dot(keys, query[:, lanes], preferred_element_type=WIDE)
        probs = jnp.exp(scores - log_ref[0, :, lanes])
        grad_probs = jnp.dot(values, grad_out, preferred_element_type=WIDE)
        along = jnp.sum(grad_out.astype(WIDE) * wide_ref[:, lanes], axis=0, keepdims=True)
        grad_scores = (probs * (grad_probs - along)).astype(LOW)
        grad_query = jnp.dot(keys_t, grad_scores, preferred_element_type=WIDE) * SCALE
        out_ref[0, :, lanes] = grad_query.astype(LOW)
        grad_keys += jnp.dot(
            grad_scores, both[lanes, :HEAD_DIM], preferred_element_type=WIDE
        )
        grad_values += jnp.dot(
            probs.astype(LOW), both[lanes, HEAD_DIM:], preferred_element_type=WIDE
        )
    joined = jnp.concatenate((grad_keys * SCALE, grad_values), axis=1).T
    out_ref[1] = joined[:HEAD_DIM].astype(LOW)
    out_ref[2] = joined[HEAD_DIM:].astype(LOW)


def attend_backward(
    query, keys, values, grad_out, wide, log_total, mask, ones, first_head, count, before=()
):
    cols, rows = query.shape
    head = pl.BlockSpec((HEAD_DIM, rows), lambda h: (h + first_head, 0))
    shared = pl.BlockSpec((HEAD_DIM, rows), lambda h: (0, 0))
    return pl.pallas_call(
        attend_backward_body,
        grid=(count,),
        in_specs=[
            head,
            head,
            head,
            head,
            head,
            pl.BlockSpec((1, 1, rows), lambda h: (h + first_head, 0, 0)),
            shared,
            shared,
        ]
        + [pl.BlockSpec(memory_space=pl.ANY)] * len(before),
        out_specs=pl.BlockSpec((3, HEAD_DIM, rows), lambda h: (0, h + first_head, 0)),
        out_shape=jax.ShapeDtypeStruct((3, cols, rows), LOW),
        input_output_aliases={8 + k: k for k in range(len(before))},
        compiler_params=pltpu.CompilerParams(vmem_limit_bytes=40 * 1024 * 1024),
        cost_estimate=pl.CostEstimate(
            flops=56 * count * rows * rows * HEAD_DIM,
            bytes_accessed=20 * count * HEAD_DIM * rows,
            transcendentals=count * rows * rows,
        ),
    )(query, keys, values, grad_out, wide, log_total, mask, ones, *before)


def forward_body(
    near_ref, far_ref, expand_ref, shrink_ref, bias_ref, hidden_ref, slope_ref, kept_ref, sent_ref
):
    def work(rows_ref, down_ref):
        preact = jnp.dot(rows_ref[...], expand_ref[...], preferred_element_type=WIDE)
        preact = preact + bias_ref[...]
        share = 0.5 * (1.0 + lax.erf(preact * 0.5**0.5))
        hidden = (preact * share).astype(LOW)
        hidden_ref[...] = hidden
        bell = jnp.exp(preact * preact * -0.5) * (0.5 / math.pi) ** 0.5
        slope_ref[...] = share + preact * bell
        down_ref[...] = times_t(hidden, shrink_ref[...]).astype(down_ref.dtype)

    @pl.when(pl.program_id(0) < 2)
    def _():
        work(far_ref, sent_ref)

    @pl.when(pl.program_id(0) >= 2)
    def _():
        work(near_ref, kept_ref)


def backward_body(
    near_ref, far_ref, expand_ref, shrink_ref, slope_ref, pre_ref, kept_ref, sent_ref, sum_ref
):
    def work(rows_ref, back_ref):
        grad_hidden = jnp.dot(rows_ref[...], shrink_ref[...], preferred_element_type=WIDE)
        grad_pre = (grad_hidden * slope_ref[...]).astype(LOW)
        pre_ref[...] = grad_pre
        back_ref[...] = times_t(grad_pre, expand_ref[...]).astype(back_ref.dtype)
        sums = jnp.sum(grad_pre.astype(WIDE), axis=0, keepdims=True)

        @pl.when(pl.program_id(0) == 0)
        def _():
            sum_ref[...] = sums

        @pl.when(pl.program_id(0) != 0)
        def _():
            sum_ref[...] += sums

    @pl.when(pl.program_id(0) < 2)
    def _():
        work(far_ref, sent_ref)

    @pl.when(pl.program_id(0) >= 2)
    def _():
        work(near_ref, kept_ref)


def hidden_specs(rows, width, cols):
    step = rows // 2
    near = pl.BlockSpec((step, width), lambda r: (jnp.maximum(r - 2, 0), 0))
    far = pl.BlockSpec((step, width), lambda r: (jnp.minimum(r, 1), 0))
    units = pl.BlockSpec((step, cols), lambda r: ((r + 2) % 4, 0))
    expand = pl.BlockSpec((width, cols), lambda r: (0, 0))
    shrink = pl.BlockSpec((width, cols), lambda r: (0, 1))
    line = pl.BlockSpec((1, cols), lambda r: (0, 0))
    return near, far, units, expand, shrink, line


def hidden_cost(rows, width, cols):
    return pl.CostEstimate(
        flops=16 * rows * cols * width,
        bytes_accessed=10 * rows * width + 12 * rows * cols + 4 * width * cols,
        transcendentals=4 * rows * cols,
    )


def hidden_forward(near_rows, far_rows, weights, bias):
    rows, width = near_rows.shape
    cols = weights.shape[1] // 2
    near, far, units, expand, shrink, line = hidden_specs(rows, width, cols)
    return pl.pallas_call(
        forward_body,
        grid=(4,),
        in_specs=[near, far, expand, shrink, line],
        out_specs=[units, units, near, far],
        out_shape=[
            jax.ShapeDtypeStruct((2 * rows, cols), LOW),
            jax.ShapeDtypeStruct((2 * rows, cols), WIDE),
            jax.ShapeDtypeStruct((rows, width), WIDE),
            jax.ShapeDtypeStruct((rows, width), LOW),
        ],
        compiler_params=pltpu.CompilerParams(vmem_limit_bytes=40 * 1024 * 1024),
        cost_estimate=hidden_cost(rows, width, cols),
    )(near_rows, far_rows, weights, weights, bias)


def hidden_backward(near_rows, far_rows, weights, slope):
    rows, width = near_rows.shape
    cols = weights.shape[1] // 2
    near, far, units, expand, shrink, line = hidden_specs(rows, width, cols)
    return pl.pallas_call(
        backward_body,
        grid=(4,),
        in_specs=[near, far, expand, shrink, units],
        out_specs=[units, near, far, line],
        out_shape=[
            jax.ShapeDtypeStruct((2 * rows, cols), LOW),
            jax.ShapeDtypeStruct((rows, width), WIDE),
            jax.ShapeDtypeStruct((rows, width), LOW),
            jax.ShapeDtypeStruct((1, cols), WIDE),
        ],
        compiler_params=pltpu.CompilerParams(vmem_limit_bytes=40 * 1024 * 1024),
        cost_estimate=hidden_cost(rows, width, cols),
    )(near_rows, far_rows, weights, weights, slope)


def turned_slot(slot, count):
    turned = slot * 0
    while count > 1:
        turned = turned * 2 + slot % 2
        slot = slot // 2
        count //= 2
    return turned


def far_first(total, tiles):
    order = jnp.array([turned_slot(slot, tiles) for slot in range(tiles)])
    parts = total.reshape(tiles, -1, total.shape[1])
    parts = jnp.take(parts, order ^ lax.axis_index("gy"), axis=0).reshape(total.shape)
    half = total.shape[0] // 2
    return parts[:half], parts[half:].astype(LOW)


def unit_grads_body(
    gn_ref, gf_ref, sn_ref, sf_ref, hidden_ref, pre_ref, out_ref
):
    half = gn_ref.shape[0]

    def work(near_ref, far_ref, units_ref):
        total = inner_rows(near_ref[...], units_ref[:half])
        total += inner_rows(far_ref[...], units_ref[half:])
        out_ref[...] = total.astype(LOW)

    @pl.when(pl.program_id(0) < 4)
    def _():
        work(gn_ref, gf_ref, hidden_ref)

    @pl.when(pl.program_id(0) >= 4)
    def _():
        work(sn_ref, sf_ref, pre_ref)


def unit_grads(grad_near, grad_far, second_near, second_far, hidden, grad_pre):
    half, width = grad_near.shape
    rows, cols = hidden.shape
    tile = width // 4
    early = pl.BlockSpec((half, tile), lambda r: (0, jnp.minimum(r, 3)))
    late = pl.BlockSpec((half, tile), lambda r: (0, jnp.maximum(r - 4, 0)))
    whole = pl.BlockSpec((rows, cols), lambda r: (0, 0))
    return pl.pallas_call(
        unit_grads_body,
        grid=(8,),
        in_specs=[early, early, late, late, whole, whole],
        out_specs=pl.BlockSpec((tile, cols), lambda r: (r % 4, r // 4)),
        out_shape=jax.ShapeDtypeStruct((width, 2 * cols), LOW),
        compiler_params=pltpu.CompilerParams(vmem_limit_bytes=40 * 1024 * 1024),
        cost_estimate=pl.CostEstimate(
            flops=8 * rows * cols * width,
            bytes_accessed=4 * rows * (width + cols) + 4 * width * cols,
            transcendentals=0,
        ),
    )(grad_near, grad_far, second_near, second_far, hidden, grad_pre)


def project_body(rows_ref, weight_ref, kept_ref, sent_ref, turned_ref):
    @pl.when(pl.program_id(0) == 0)
    def _():
        turned_ref[...] = rows_ref[...].T

    total = times_t(turned_ref[...], weight_ref[...])
    half = kept_ref.shape[0]
    kept_ref[...] = total[:half]
    sent_ref[...] = total[half:].astype(LOW)


def project_rows(values, weight):
    cols, rows = values.shape
    width = weight.shape[0]
    tile = width // 4
    return pl.pallas_call(
        project_body,
        grid=(4,),
        in_specs=[
            pl.BlockSpec((cols, rows), lambda t: (0, 0)),
            pl.BlockSpec((tile, cols), lambda t: (t, 0)),
        ],
        out_specs=[
            pl.BlockSpec((rows // 2, tile), lambda t: (0, t)),
            pl.BlockSpec((rows // 2, tile), lambda t: (0, t)),
        ],
        out_shape=[
            jax.ShapeDtypeStruct((rows // 2, width), WIDE),
            jax.ShapeDtypeStruct((rows // 2, width), LOW),
        ],
        scratch_shapes=[pltpu.VMEM((rows, cols), LOW)],
        compiler_params=pltpu.CompilerParams(vmem_limit_bytes=40 * 1024 * 1024),
        cost_estimate=pl.CostEstimate(
            flops=2 * rows * cols * width,
            bytes_accessed=2 * rows * cols + 2 * width * cols + 3 * rows * width,
            transcendentals=0,
        ),
    )(values, weight)


def head_grads_body(place_ref, fn_ref, ff_ref, gn_ref, gf_ref, mixed_ref, attended_ref, out_ref):
    cols = mixed_ref.shape[0]
    first = jnp.concatenate((fn_ref[...], ff_ref[...]), axis=0)
    grad = jnp.concatenate((gn_ref[...], gf_ref[...]), axis=0)
    out_ref[:, :cols] = times(mixed_ref[...], first).T.astype(out_ref.dtype)
    out_ref[:, cols:] = times(attended_ref[...], grad).T.astype(out_ref.dtype)


def head_grads_of(first_near, first_far, grad_near, grad_far, mixed, attended, upper):
    half, width = first_near.shape
    rows = 2 * half
    cols, more = mixed.shape[0], attended.shape[0]
    tiles = lax.axis_size("gy")
    tile = width // tiles
    dtype = LOW if upper else WIDE
    if tile % 128:
        first = jnp.concatenate((first_near, first_far), axis=0)
        grad = jnp.concatenate((grad_near, grad_far), axis=0)
        total = jnp.concatenate((times(mixed, first).T, times(attended, grad).T), axis=1)
        return far_first(total, tiles)[1 if upper else 0].astype(dtype)
    start = tiles // 2 if upper else 0

    def block(r, place):
        return turned_slot(r + start, tiles) ^ place[0]

    narrow = pl.BlockSpec((half, tile), lambda r, place: (0, block(r, place)))
    return pl.pallas_call(
        head_grads_body,
        grid_spec=pltpu.PrefetchScalarGridSpec(
            num_scalar_prefetch=1,
            grid=(tiles // 2,),
            in_specs=[
                narrow,
                narrow,
                narrow,
                narrow,
                pl.BlockSpec((cols, rows), lambda r, place: (0, 0)),
                pl.BlockSpec((more, rows), lambda r, place: (0, 0)),
            ],
            out_specs=pl.BlockSpec((tile, cols + more), lambda r, place: (r, 0)),
        ),
        out_shape=jax.ShapeDtypeStruct((width // 2, cols + more), dtype),
        compiler_params=pltpu.CompilerParams(vmem_limit_bytes=40 * 1024 * 1024),
        cost_estimate=pl.CostEstimate(
            flops=2 * rows * (cols + more) * width,
            bytes_accessed=2 * rows * (width + cols + more) + 2 * width * (cols + more),
            transcendentals=0,
        ),
    )(
        lax.axis_index("gy").astype(jnp.int32)[None],
        first_near,
        first_far,
        grad_near,
        grad_far,
        mixed,
        attended,
    )


def on_device(
    tokens,
    project_in,
    query_bias,
    value_bias,
    project_out,
    output_bias,
    attention_scale,
    first_norm_gain,
    first_norm_bias,
    second_norm_gain,
    second_norm_bias,
    expand_weight,
    expand_bias,
    shrink_weight,
    shrink_bias,
    feedforward_scale,
    cotangent,
):
    nx, ny = lax.axis_size("gx"), lax.axis_size("gy")
    head_cols = project_out.shape[0]
    hidden_cols = expand_weight.shape[1]
    packed_shape = tokens.shape
    block = -(-SEQ // (nx * 16)) * 16
    column = jnp.arange(block)
    mask = jnp.concatenate(
        [
            jnp.where((lax.axis_index("gx") ^ k) * block + column < SEQ, 0.0, -1e30)
            for k in slot_blocks(nx)
        ]
    )
    top = jnp.arange(HEAD_DIM)[:, None] == 0
    mask = jnp.where(top, mask[None], 0.0).astype(LOW)
    ones = jnp.where(top, jnp.ones((1, nx * block), WIDE), 0.0).astype(LOW)

    small = jnp.concatenate(
        pieces(
            jnp.stack(
                (
                    output_bias,
                    attention_scale,
                    first_norm_gain,
                    first_norm_bias,
                    second_norm_gain,
                    second_norm_bias,
                    shrink_bias,
                    feedforward_scale,
                )
            ),
            3,
        ),
        axis=0,
    )
    weight_in = lax.all_gather(project_in.reshape(-1, 3 * head_cols), "gy", axis=0, tiled=True)
    units_weight = jnp.concatenate((expand_weight, shrink_weight.T), axis=1)

    parts = to_rows(
        jnp.concatenate((spread_images(tokens, block), spread_images(cotangent, block)), axis=2)
    )
    input_parts = cross(parts[:, :block], jnp.broadcast_to(small[None], (ny,) + small.shape))
    input_parts, grad_parts, units_weight, weight_out = together(
        input_parts, parts[:, block:], units_weight, project_out.T
    )
    input_parts, small = input_parts[:, :block], input_parts[:, block : block + 24]
    grad_parts = cross(grad_parts)
    weight_out = gather_weight(weight_out)
    units_weight = lax.all_gather(units_weight, "gy", axis=0, tiled=True)
    small = small.astype(WIDE)
    small = small[:, :8] + (small[:, 8:16] + small[:, 16:])
    out_shift, attn_scale, gain_one, shift_one, gain_two, shift_two, shrink_shift, ff_scale = [
        small[:, k].reshape(D) for k in range(8)
    ]
    inputs = join_width(input_parts).astype(WIDE)

    first, first_hat, first_rstd = norm_forward(inputs, gain_one, shift_one)
    first_near = gather_step(first)
    first_other = swap(first_near, "gx", 1)
    first_all = jnp.concatenate((first_near, first_other), axis=0)
    mixed = lax.dot_general(
        weight_in, first_all, (((0,), (1,)), ((), ())), preferred_element_type=WIDE
    )
    query = (mixed[:head_cols] + query_bias[:, None]).astype(LOW)
    keys = mixed[head_cols : 2 * head_cols].astype(LOW)
    values = (mixed[2 * head_cols :] + value_bias[:, None]).astype(LOW)
    heads = head_cols // HEAD_DIM
    half = attend_forward(query, keys, values, mask, ones, 0, heads // 2)
    *half, grad_parts = together(*half, grad_parts)
    grad = join_width(grad_parts).astype(WIDE)
    grad_b = grad * ff_scale
    grad_b_own, grad_b_other = gather_far(grad_b.astype(LOW))
    attended, attended_wide, log_total = attend_forward(
        query, keys, values, mask, ones, heads // 2, heads - heads // 2, half
    )
    attended, grad_b_other = together(attended, grad_b_other)
    grad_b_near = jnp.concatenate((grad_b_own, grad_b_other), axis=0)
    grad_b_far = swap(grad_b_near, "gx", 1)

    kept, sent = project_rows(attended, weight_out)
    branch_a = scatter_far(scatter_near(kept, sent)) + out_shift
    middle = inputs + attn_scale * branch_a
    second, second_hat, second_rstd = norm_forward(middle, gain_two, shift_two)
    second_near, second_far = gather_halves(second)
    hidden, slope, kept_b, sent_b = hidden_forward(
        second_near, second_far, units_weight, expand_bias[None]
    )
    grad_pre, kept, sent, pre_sum = hidden_backward(grad_b_near, grad_b_far, units_weight, slope)
    wide_grads = unit_grads(grad_b_near, grad_b_far, second_near, second_far, hidden, grad_pre)
    grad_second, received = scatter_last(scatter_near(kept, sent))
    received, wide_grads = together(received, wide_grads)
    grad_second = grad_second + received.astype(WIDE)
    wide_grads = lax.psum_scatter(wide_grads, "gy", scatter_dimension=0, tiled=True)

    grad_middle = grad + norm_backward(grad_second, gain_two, second_hat, second_rstd)
    grad_a = grad_middle * attn_scale
    grad_a_own, grad_a_other = gather_far(grad_a.astype(LOW))
    branch_near = scatter_near(kept_b, sent_b)
    grad_a_other, branch_near = together(grad_a_other, branch_near)
    grad_a_near = jnp.concatenate((grad_a_own, grad_a_other), axis=0)
    grad_a_other = swap(grad_a_near, "gx", 1)
    grad_a_all = jnp.concatenate((grad_a_near, grad_a_other), axis=0)
    branch_kept, branch_far = scatter_last(branch_near)
    grad_attended = lax.dot_general(
        weight_out, grad_a_all, (((0,), (1,)), ((), ())), preferred_element_type=WIDE
    ).astype(LOW)
    half = attend_backward(
        query, keys, values, grad_attended, attended_wide, log_total, mask, ones, 0, heads // 2
    )
    half, branch_far = together(half, branch_far)
    grad_mixed = attend_backward(
        query,
        keys,
        values,
        grad_attended,
        attended_wide,
        log_total,
        mask,
        ones,
        heads // 2,
        heads - heads // 2,
        (half,),
    )
    branch_b = branch_kept + branch_far.astype(WIDE) + shrink_shift
    output_parts = cut_width((middle + ff_scale * branch_b).astype(LOW))
    joined = grad_mixed.reshape(3 * head_cols, nx * block)
    kept, sent = project_rows(joined, weight_in)
    shares = (first_near, first_other, grad_a_near, grad_a_other, joined, attended)
    received, head_sent, output_parts = together(
        swap(sent, "gx", 1), head_grads_of(*shares, True), output_parts
    )
    grad_first, received = scatter_last(kept + received.astype(WIDE))
    received, head_other, head_kept, wide_grads = together(
        received, swap(head_sent, "gy", 1), head_grads_of(*shares, False), wide_grads
    )
    grad_first = grad_first + received.astype(WIDE)
    wide_grads = wide_grads.astype(WIDE)
    head_kept, head_other = scatter_step(head_kept + head_other.astype(WIDE), 2)
    input_gradient = grad_middle + norm_backward(grad_first, gain_one, first_hat, first_rstd)
    sums = jnp.stack(
        [
            jnp.sum(item, axis=0)
            for item in (
                grad_a,
                grad_middle * branch_a,
                grad_first * first_hat,
                grad_first,
                grad_second * second_hat,
                grad_second,
                grad_b,
                grad * branch_b,
            )
        ]
    )
    image_sums = jnp.concatenate(
        (
            jnp.sum(grad_mixed[0].astype(WIDE), axis=1),
            jnp.sum(grad_mixed[2].astype(WIDE), axis=1),
            pre_sum[0],
        )
    )
    input_parts = cut_width(input_gradient.astype(LOW))
    input_parts, output_parts = together(input_parts, cross(output_parts))
    input_parts = cross(input_parts, split_lines(sums), spread_lines(image_sums))
    input_parts, head_other = together(input_parts, head_other)
    head_grads = head_kept + head_other.astype(WIDE)
    bit = 4
    while bit < ny:
        head_kept, head_other = scatter_step(head_grads, bit)
        head_grads = head_kept + head_other.astype(WIDE)
        bit *= 2
    both = to_images(jnp.concatenate((input_parts[:, :block], output_parts), axis=1))
    block_output = join_images(both[:, :, block:], packed_shape)
    input_gradient = join_images(both[:, :, :block], packed_shape).astype(WIDE)
    sums = over_rows(sum_lines(input_parts[:, block : block + 16]))
    lines = 2 * image_sums.shape[0] * ny // D
    image_sums = sum_lines(input_parts[:, block + 16 : block + 16 + lines]).reshape(-1)
    head_sums, pre_sum = image_sums[: 2 * head_cols], image_sums[2 * head_cols :]
    return (
        block_output,
        input_gradient,
        head_grads[:, : 3 * head_cols].reshape(-1, 3, head_cols),
        head_sums[:head_cols],
        head_sums[head_cols:],
        head_grads[:, 3 * head_cols :].T,
        sums[0],
        sums[1],
        sums[2],
        sums[3],
        sums[4],
        sums[5],
        wide_grads[:, hidden_cols:],
        pre_sum,
        wide_grads[:, :hidden_cols].T,
        sums[6],
        sums[7],
    )


def solution(mesh):
    rows = P("gx", "gy", None)
    wide, heads = P("gy"), P("gx")
    placed = (
        rows, P("gy", None, "gx"), heads, heads, P("gx", "gy"), wide, wide, wide, wide, wide, wide,
        P("gy", "gx"), heads, P("gx", "gy"), wide, wide, rows,
    )
    results = (
        rows, rows, P("gy", None, "gx"), heads, heads, P("gx", "gy"), wide, wide, wide, wide, wide,
        wide, P("gy", "gx"), heads, P("gx", "gy"), wide, wide,
    )
    return jax.shard_map(
        on_device, mesh=mesh, in_specs=placed, out_specs=results, check_vma=False
    )
```

```python
import math

import jax
import jax.numpy as jnp
from jax import lax
from jax.experimental import pallas as pl
from jax.experimental.pallas import tpu as pltpu
from jax.sharding import PartitionSpec as P

D = 1024
HEAD_DIM = 64
SEQ = 1370
SCALE = HEAD_DIM ** (-0.5)
LOW = jnp.bfloat16
WIDE = jnp.float32


def swap(values, axis, bit):
    size = lax.axis_size(axis)
    return lax.ppermute(values, axis, [(k, k ^ bit) for k in range(size)])


def together(*values):
    return lax.optimization_barrier(values)


def gather_far(values):
    bit = lax.axis_size("gx") // 2
    while bit > 2:
        values = jnp.concatenate((values, swap(values, "gx", bit)), axis=0)
        bit //= 2
    return values, swap(values, "gx", 2)


def gather_step(values):
    return jnp.concatenate(gather_far(values), axis=0)


def gather_halves(values):
    near = gather_step(values)
    return near, swap(near, "gx", 1)


def slot_blocks(count):
    order = [0]
    bit = count // 2
    while bit:
        order = order + [k ^ bit for k in order]
        bit //= 2
    return order


def scatter_near(kept, sent):
    return kept + swap(sent, "gx", 1).astype(WIDE)


def scatter_last(partial):
    bit = 2
    while True:
        half = partial.shape[0] // 2
        received = swap(partial[half:].astype(LOW), "gx", bit)
        partial = partial[:half]
        bit *= 2
        if bit >= lax.axis_size("gx"):
            return partial, received
        partial = partial + received.astype(WIDE)


def scatter_far(partial):
    kept, received = scatter_last(partial)
    return kept + received.astype(WIDE)


def scatter_step(total, bit):
    half = total.shape[0] // 2
    return total[:half], swap(total[half:].astype(LOW), "gy", bit)


def pieces(values, count):
    parts = []
    for _ in range(count):
        head = lax.reduce_precision(values, exponent_bits=8, mantissa_bits=7)
        parts.append(head.astype(LOW))
        values = values - head
    return parts


def spread_images(values, block):
    nx, ny = lax.axis_size("gx"), lax.axis_size("gy")
    images = values.reshape(ny // nx, SEQ, D // ny)
    images = jnp.pad(images, ((0, 0), (0, nx * block - SEQ), (0, 0)))
    return images.reshape(ny // nx, nx, block, D // ny).transpose(1, 0, 2, 3)


def to_rows(parts):
    parts = lax.all_to_all(parts, "gx", split_axis=0, concat_axis=0, tiled=True)
    return parts.reshape((-1,) + parts.shape[2:])


def to_images(parts):
    nx, ny = lax.axis_size("gx"), lax.axis_size("gy")
    parts = parts.reshape((nx, ny // nx) + parts.shape[1:])
    return lax.all_to_all(parts, "gx", split_axis=0, concat_axis=0, tiled=True)


def trade_images(parts):
    nx, ny = lax.axis_size("gx"), lax.axis_size("gy")
    place = lax.axis_index("gx")
    shape = (nx, ny // nx) + parts.shape[1:]
    bit = 1
    while bit < nx:
        pair = parts.reshape((nx // (2 * bit), 2, bit) + shape[1:])
        upper = (place & bit) != 0
        mine = jnp.where(upper, pair[:, 1], pair[:, 0])
        theirs = swap(jnp.where(upper, pair[:, 0], pair[:, 1]), "gx", bit)
        low, high = jnp.where(upper, theirs, mine), jnp.where(upper, mine, theirs)
        parts = jnp.stack((low, high), axis=1).reshape(shape)
        bit *= 2
    return parts


def join_images(parts, packed_shape):
    nx, per, block, width = parts.shape
    parts = parts.transpose(1, 0, 2, 3).reshape(per, nx * block, width)
    return parts[:, :SEQ].reshape(packed_shape)


def over_rows(sums):
    bit = 1
    while bit < lax.axis_size("gx"):
        sums = sums + swap(sums, "gx", bit)
        bit *= 2
    return sums


def cross(parts, *extra):
    if extra:
        rows = sum(item.shape[1] for item in extra)
        space = jnp.zeros((parts.shape[0], -rows % 16, parts.shape[2]), LOW)
        parts = jnp.concatenate((parts, *extra, space), axis=1)
    return lax.all_to_all(parts, "gy", split_axis=0, concat_axis=0, tiled=True)


def spread_lines(values):
    ny = lax.axis_size("gy")
    lines = jnp.concatenate([item.reshape(-1, D // ny) for item in pieces(values, 2)], axis=0)
    return jnp.broadcast_to(lines[None], (ny,) + lines.shape)


def split_lines(vectors):
    ny = lax.axis_size("gy")
    lines = jnp.concatenate(pieces(vectors, 2), axis=0)
    return lines.reshape(-1, ny, D // ny).transpose(1, 0, 2)


def sum_lines(lines):
    return jnp.sum(lines.astype(WIDE), axis=0).reshape(2, -1, lines.shape[2]).sum(axis=0)


def join_width(parts):
    return parts.transpose(1, 0, 2).reshape(parts.shape[1], D)


def cut_width(values):
    ny = lax.axis_size("gy")
    return values.reshape(values.shape[0], ny, D // ny).transpose(1, 0, 2)


def gather_weight(weight):
    place = lax.axis_index("gy")
    rows, cols = weight.shape
    weight = weight[None]
    bit = lax.axis_size("gy") // 2
    while bit:
        other = swap(weight, "gy", bit)
        upper = (place & bit) != 0
        low, high = jnp.where(upper, other, weight), jnp.where(upper, weight, other)
        weight = jnp.stack((low, high), axis=1).reshape(-1, rows, cols)
        bit //= 2
    return weight.reshape(-1, cols)


def norm_forward(values, gain, shift):
    center = jnp.mean(values, axis=1, keepdims=True)
    spread = jnp.mean(values * values, axis=1, keepdims=True) - center * center
    rstd = lax.rsqrt(spread + 1e-06)
    normed = (values - center) * rstd
    return (normed * gain + shift).astype(LOW), normed, rstd


def norm_backward(grad, gain, normed, rstd):
    scaled = grad * gain
    total = jnp.mean(scaled, axis=1, keepdims=True)
    along = jnp.mean(scaled * normed, axis=1, keepdims=True)
    return rstd * (scaled - total - normed * along)


def times(left, right):
    return jnp.dot(left, right, preferred_element_type=WIDE)


def times_t(left, right):
    return lax.dot_general(left, right, (((1,), (1,)), ((), ())), preferred_element_type=WIDE)


def inner_rows(left, right):
    return lax.dot_general(left, right, (((0,), (0,)), ((), ())), preferred_element_type=WIDE)


def lane_blocks(size):
    return [(start, min(256, size - start)) for start in range(0, size, 256)]


def with_row(head, row):
    return jnp.concatenate((head, row), axis=0)


def attend_forward_body(q_ref, k_ref, v_ref, mask_ref, ones_ref, *refs):
    low_ref, wide_ref, log_ref = refs[-3:]
    keys = with_row(k_ref[...], mask_ref[...]).T
    query = with_row((q_ref[...].astype(WIDE) * SCALE).astype(LOW), ones_ref[...])
    values = with_row(v_ref[...], ones_ref[...])
    for start, size in lane_blocks(query.shape[1]):
        lanes = slice(start, start + size)
        scores = jnp.dot(keys, query[:, lanes], preferred_element_type=WIDE)
        peak = jnp.max(scores, axis=0, keepdims=True)
        raised = jnp.exp(scores - peak).astype(LOW)
        mixed = jnp.dot(values, raised, preferred_element_type=WIDE)
        total = mixed[HEAD_DIM : HEAD_DIM + 1]
        attended = mixed[:HEAD_DIM] / total
        wide_ref[:, lanes] = attended
        low_ref[:, lanes] = attended.astype(LOW)
        log_ref[0, :, lanes] = peak + jnp.log(total)


def attend_forward(query, keys, values, mask, ones, first_head, count, before=()):
    cols, rows = query.shape
    heads = cols // HEAD_DIM
    head = pl.BlockSpec((HEAD_DIM, rows), lambda h: (h + first_head, 0))
    shared = pl.BlockSpec((HEAD_DIM, rows), lambda h: (0, 0))
    return pl.pallas_call(
        attend_forward_body,
        grid=(count,),
        in_specs=[head, head, head, shared, shared] + [pl.BlockSpec(memory_space=pl.ANY)] * len(before),
        out_specs=[head, head, pl.BlockSpec((1, 1, rows), lambda h: (h + first_head, 0, 0))],
        out_shape=[
            jax.ShapeDtypeStruct((cols, rows), LOW),
            jax.ShapeDtypeStruct((cols, rows), WIDE),
            jax.ShapeDtypeStruct((heads, 1, rows), WIDE),
        ],
        input_output_aliases={5 + k: k for k in range(len(before))},
        compiler_params=pltpu.CompilerParams(vmem_limit_bytes=40 * 1024 * 1024),
        cost_estimate=pl.CostEstimate(
            flops=48 * count * rows * rows * HEAD_DIM,
            bytes_accessed=12 * count * HEAD_DIM * rows,
            transcendentals=count * rows * rows,
        ),
    )(query, keys, values, mask, ones, *before)


def attend_backward_body(
    q_ref, k_ref, v_ref, g_ref, wide_ref, log_ref, mask_ref, ones_ref, *refs
):
    out_ref = refs[-1]
    rows = q_ref.shape[1]
    keys_t = k_ref[...]
    keys = with_row(keys_t, mask_ref[...]).T
    query = with_row((q_ref[...].astype(WIDE) * SCALE).astype(LOW), ones_ref[...])
    values = with_row(v_ref[...], mask_ref[...]).T[:, :HEAD_DIM]
    both = with_row(q_ref[...], g_ref[...]).T
    grad_keys = jnp.zeros((rows, HEAD_DIM), WIDE)
    grad_values = jnp.zeros((rows, HEAD_DIM), WIDE)
    for start, size in lane_blocks(rows):
        lanes = slice(start, start + size)
        grad_out = g_ref[:, lanes]
        scores = jnp.dot(keys, query[:, lanes], preferred_element_type=WIDE)
        probs = jnp.exp(scores - log_ref[0, :, lanes])
        grad_probs = jnp.dot(values, grad_out, preferred_element_type=WIDE)
        along = jnp.sum(grad_out.astype(WIDE) * wide_ref[:, lanes], axis=0, keepdims=True)
        grad_scores = (probs * (grad_probs - along)).astype(LOW)
        grad_query = jnp.dot(keys_t, grad_scores, preferred_element_type=WIDE) * SCALE
        out_ref[0, :, lanes] = grad_query.astype(LOW)
        grad_keys += jnp.dot(
            grad_scores, both[lanes, :HEAD_DIM], preferred_element_type=WIDE
        )
        grad_values += jnp.dot(
            probs.astype(LOW), both[lanes, HEAD_DIM:], preferred_element_type=WIDE
        )
    joined = jnp.concatenate((grad_keys * SCALE, grad_values), axis=1).T
    out_ref[1] = joined[:HEAD_DIM].astype(LOW)
    out_ref[2] = joined[HEAD_DIM:].astype(LOW)


def attend_backward(
    query, keys, values, grad_out, wide, log_total, mask, ones, first_head, count, before=()
):
    cols, rows = query.shape
    head = pl.BlockSpec((HEAD_DIM, rows), lambda h: (h + first_head, 0))
    shared = pl.BlockSpec((HEAD_DIM, rows), lambda h: (0, 0))
    return pl.pallas_call(
        attend_backward_body,
        grid=(count,),
        in_specs=[
            head,
            head,
            head,
            head,
            head,
            pl.BlockSpec((1, 1, rows), lambda h: (h + first_head, 0, 0)),
            shared,
            shared,
        ]
        + [pl.BlockSpec(memory_space=pl.ANY)] * len(before),
        out_specs=pl.BlockSpec((3, HEAD_DIM, rows), lambda h: (0, h + first_head, 0)),
        out_shape=jax.ShapeDtypeStruct((3, cols, rows), LOW),
        input_output_aliases={8 + k: k for k in range(len(before))},
        compiler_params=pltpu.CompilerParams(vmem_limit_bytes=40 * 1024 * 1024),
        cost_estimate=pl.CostEstimate(
            flops=56 * count * rows * rows * HEAD_DIM,
            bytes_accessed=20 * count * HEAD_DIM * rows,
            transcendentals=count * rows * rows,
        ),
    )(query, keys, values, grad_out, wide, log_total, mask, ones, *before)


def forward_body(
    near_ref, far_ref, expand_ref, shrink_ref, bias_ref, hidden_ref, slope_ref, kept_ref, sent_ref
):
    def work(rows_ref, down_ref):
        preact = jnp.dot(rows_ref[...], expand_ref[...], preferred_element_type=WIDE)
        preact = preact + bias_ref[...]
        share = 0.5 * (1.0 + lax.erf(preact * 0.5**0.5))
        hidden = (preact * share).astype(LOW)
        hidden_ref[...] = hidden
        bell = jnp.exp(preact * preact * -0.5) * (0.5 / math.pi) ** 0.5
        slope_ref[...] = share + preact * bell
        down_ref[...] = times_t(hidden, shrink_ref[...]).astype(down_ref.dtype)

    @pl.when(pl.program_id(0) < 2)
    def _():
        work(far_ref, sent_ref)

    @pl.when(pl.program_id(0) >= 2)
    def _():
        work(near_ref, kept_ref)


def backward_body(
    near_ref, far_ref, expand_ref, shrink_ref, slope_ref, pre_ref, kept_ref, sent_ref, sum_ref
):
    def work(rows_ref, back_ref):
        grad_hidden = jnp.dot(rows_ref[...], shrink_ref[...], preferred_element_type=WIDE)
        grad_pre = (grad_hidden * slope_ref[...]).astype(LOW)
        pre_ref[...] = grad_pre
        back_ref[...] = times_t(grad_pre, expand_ref[...]).astype(back_ref.dtype)
        sums = jnp.sum(grad_pre.astype(WIDE), axis=0, keepdims=True)

        @pl.when(pl.program_id(0) == 0)
        def _():
            sum_ref[...] = sums

        @pl.when(pl.program_id(0) != 0)
        def _():
            sum_ref[...] += sums

    @pl.when(pl.program_id(0) < 2)
    def _():
        work(far_ref, sent_ref)

    @pl.when(pl.program_id(0) >= 2)
    def _():
        work(near_ref, kept_ref)


def hidden_specs(rows, width, cols):
    step = rows // 2
    near = pl.BlockSpec((step, width), lambda r: (jnp.maximum(r - 2, 0), 0))
    far = pl.BlockSpec((step, width), lambda r: (jnp.minimum(r, 1), 0))
    units = pl.BlockSpec((step, cols), lambda r: ((r + 2) % 4, 0))
    expand = pl.BlockSpec((width, cols), lambda r: (0, 0))
    shrink = pl.BlockSpec((width, cols), lambda r: (0, 1))
    line = pl.BlockSpec((1, cols), lambda r: (0, 0))
    return near, far, units, expand, shrink, line


def hidden_cost(rows, width, cols):
    return pl.CostEstimate(
        flops=16 * rows * cols * width,
        bytes_accessed=10 * rows * width + 12 * rows * cols + 4 * width * cols,
        transcendentals=4 * rows * cols,
    )


def hidden_forward(near_rows, far_rows, weights, bias):
    rows, width = near_rows.shape
    cols = weights.shape[1] // 2
    near, far, units, expand, shrink, line = hidden_specs(rows, width, cols)
    return pl.pallas_call(
        forward_body,
        grid=(4,),
        in_specs=[near, far, expand, shrink, line],
        out_specs=[units, units, near, far],
        out_shape=[
            jax.ShapeDtypeStruct((2 * rows, cols), LOW),
            jax.ShapeDtypeStruct((2 * rows, cols), WIDE),
            jax.ShapeDtypeStruct((rows, width), WIDE),
            jax.ShapeDtypeStruct((rows, width), LOW),
        ],
        compiler_params=pltpu.CompilerParams(vmem_limit_bytes=40 * 1024 * 1024),
        cost_estimate=hidden_cost(rows, width, cols),
    )(near_rows, far_rows, weights, weights, bias)


def hidden_backward(near_rows, far_rows, weights, slope):
    rows, width = near_rows.shape
    cols = weights.shape[1] // 2
    near, far, units, expand, shrink, line = hidden_specs(rows, width, cols)
    return pl.pallas_call(
        backward_body,
        grid=(4,),
        in_specs=[near, far, expand, shrink, units],
        out_specs=[units, near, far, line],
        out_shape=[
            jax.ShapeDtypeStruct((2 * rows, cols), LOW),
            jax.ShapeDtypeStruct((rows, width), WIDE),
            jax.ShapeDtypeStruct((rows, width), LOW),
            jax.ShapeDtypeStruct((1, cols), WIDE),
        ],
        compiler_params=pltpu.CompilerParams(vmem_limit_bytes=40 * 1024 * 1024),
        cost_estimate=hidden_cost(rows, width, cols),
    )(near_rows, far_rows, weights, weights, slope)


def turned_slot(slot, count):
    turned = slot * 0
    while count > 1:
        turned = turned * 2 + slot % 2
        slot = slot // 2
        count //= 2
    return turned


def far_first(total, tiles):
    order = jnp.array([turned_slot(slot, tiles) for slot in range(tiles)])
    parts = total.reshape(tiles, -1, total.shape[1])
    parts = jnp.take(parts, order ^ lax.axis_index("gy"), axis=0).reshape(total.shape)
    half = total.shape[0] // 2
    return parts[:half], parts[half:].astype(LOW)


def unit_grads_body(
    gn_ref, gf_ref, sn_ref, sf_ref, hidden_ref, pre_ref, out_ref
):
    half = gn_ref.shape[0]

    def work(near_ref, far_ref, units_ref):
        total = inner_rows(near_ref[...], units_ref[:half])
        total += inner_rows(far_ref[...], units_ref[half:])
        out_ref[...] = total.astype(LOW)

    @pl.when(pl.program_id(0) < 4)
    def _():
        work(gn_ref, gf_ref, hidden_ref)

    @pl.when(pl.program_id(0) >= 4)
    def _():
        work(sn_ref, sf_ref, pre_ref)


def unit_grads(grad_near, grad_far, second_near, second_far, hidden, grad_pre):
    half, width = grad_near.shape
    rows, cols = hidden.shape
    tile = width // 4
    early = pl.BlockSpec((half, tile), lambda r: (0, jnp.minimum(r, 3)))
    late = pl.BlockSpec((half, tile), lambda r: (0, jnp.maximum(r - 4, 0)))
    whole = pl.BlockSpec((rows, cols), lambda r: (0, 0))
    return pl.pallas_call(
        unit_grads_body,
        grid=(8,),
        in_specs=[early, early, late, late, whole, whole],
        out_specs=pl.BlockSpec((tile, cols), lambda r: (r % 4, r // 4)),
        out_shape=jax.ShapeDtypeStruct((width, 2 * cols), LOW),
        compiler_params=pltpu.CompilerParams(vmem_limit_bytes=40 * 1024 * 1024),
        cost_estimate=pl.CostEstimate(
            flops=8 * rows * cols * width,
            bytes_accessed=4 * rows * (width + cols) + 4 * width * cols,
            transcendentals=0,
        ),
    )(grad_near, grad_far, second_near, second_far, hidden, grad_pre)


def project_body(rows_ref, weight_ref, kept_ref, sent_ref, turned_ref):
    @pl.when(pl.program_id(0) == 0)
    def _():
        turned_ref[...] = rows_ref[...].T

    total = times_t(turned_ref[...], weight_ref[...])
    half = kept_ref.shape[0]
    kept_ref[...] = total[:half]
    sent_ref[...] = total[half:].astype(LOW)


def project_rows(values, weight):
    cols, rows = values.shape
    width = weight.shape[0]
    tile = width // 4
    return pl.pallas_call(
        project_body,
        grid=(4,),
        in_specs=[
            pl.BlockSpec((cols, rows), lambda t: (0, 0)),
            pl.BlockSpec((tile, cols), lambda t: (t, 0)),
        ],
        out_specs=[
            pl.BlockSpec((rows // 2, tile), lambda t: (0, t)),
            pl.BlockSpec((rows // 2, tile), lambda t: (0, t)),
        ],
        out_shape=[
            jax.ShapeDtypeStruct((rows // 2, width), WIDE),
            jax.ShapeDtypeStruct((rows // 2, width), LOW),
        ],
        scratch_shapes=[pltpu.VMEM((rows, cols), LOW)],
        compiler_params=pltpu.CompilerParams(vmem_limit_bytes=40 * 1024 * 1024),
        cost_estimate=pl.CostEstimate(
            flops=2 * rows * cols * width,
            bytes_accessed=2 * rows * cols + 2 * width * cols + 3 * rows * width,
            transcendentals=0,
        ),
    )(values, weight)


def head_grads_body(place_ref, fn_ref, ff_ref, gn_ref, gf_ref, mixed_ref, attended_ref, out_ref):
    cols = mixed_ref.shape[0]
    first = jnp.concatenate((fn_ref[...], ff_ref[...]), axis=0)
    grad = jnp.concatenate((gn_ref[...], gf_ref[...]), axis=0)
    out_ref[:, :cols] = times(mixed_ref[...], first).T.astype(out_ref.dtype)
    out_ref[:, cols:] = times(attended_ref[...], grad).T.astype(out_ref.dtype)


def head_grads_of(first_near, first_far, grad_near, grad_far, mixed, attended, upper):
    half, width = first_near.shape
    rows = 2 * half
    cols, more = mixed.shape[0], attended.shape[0]
    tiles = lax.axis_size("gy")
    tile = width // tiles
    dtype = LOW if upper else WIDE
    if tile % 128:
        first = jnp.concatenate((first_near, first_far), axis=0)
        grad = jnp.concatenate((grad_near, grad_far), axis=0)
        total = jnp.concatenate((times(mixed, first).T, times(attended, grad).T), axis=1)
        return far_first(total, tiles)[1 if upper else 0].astype(dtype)
    start = tiles // 2 if upper else 0

    def block(r, place):
        return turned_slot(r + start, tiles) ^ place[0]

    narrow = pl.BlockSpec((half, tile), lambda r, place: (0, block(r, place)))
    return pl.pallas_call(
        head_grads_body,
        grid_spec=pltpu.PrefetchScalarGridSpec(
            num_scalar_prefetch=1,
            grid=(tiles // 2,),
            in_specs=[
                narrow,
                narrow,
                narrow,
                narrow,
                pl.BlockSpec((cols, rows), lambda r, place: (0, 0)),
                pl.BlockSpec((more, rows), lambda r, place: (0, 0)),
            ],
            out_specs=pl.BlockSpec((tile, cols + more), lambda r, place: (r, 0)),
        ),
        out_shape=jax.ShapeDtypeStruct((width // 2, cols + more), dtype),
        compiler_params=pltpu.CompilerParams(vmem_limit_bytes=40 * 1024 * 1024),
        cost_estimate=pl.CostEstimate(
            flops=2 * rows * (cols + more) * width,
            bytes_accessed=2 * rows * (width + cols + more) + 2 * width * (cols + more),
            transcendentals=0,
        ),
    )(
        lax.axis_index("gy").astype(jnp.int32)[None],
        first_near,
        first_far,
        grad_near,
        grad_far,
        mixed,
        attended,
    )


def on_device(
    tokens,
    project_in,
    query_bias,
    value_bias,
    project_out,
    output_bias,
    attention_scale,
    first_norm_gain,
    first_norm_bias,
    second_norm_gain,
    second_norm_bias,
    expand_weight,
    expand_bias,
    shrink_weight,
    shrink_bias,
    feedforward_scale,
    cotangent,
):
    nx, ny = lax.axis_size("gx"), lax.axis_size("gy")
    head_cols = project_out.shape[0]
    hidden_cols = expand_weight.shape[1]
    packed_shape = tokens.shape
    block = -(-SEQ // (nx * 16)) * 16
    column = jnp.arange(block)
    mask = jnp.concatenate(
        [
            jnp.where((lax.axis_index("gx") ^ k) * block + column < SEQ, 0.0, -1e30)
            for k in slot_blocks(nx)
        ]
    )
    top = jnp.arange(HEAD_DIM)[:, None] == 0
    mask = jnp.where(top, mask[None], 0.0).astype(LOW)
    ones = jnp.where(top, jnp.ones((1, nx * block), WIDE), 0.0).astype(LOW)

    small = jnp.concatenate(
        pieces(
            jnp.stack(
                (
                    output_bias,
                    attention_scale,
                    first_norm_gain,
                    first_norm_bias,
                    second_norm_gain,
                    second_norm_bias,
                    shrink_bias,
                    feedforward_scale,
                )
            ),
            3,
        ),
        axis=0,
    )
    weight_in = lax.all_gather(project_in.reshape(-1, 3 * head_cols), "gy", axis=0, tiled=True)
    units_weight = jnp.concatenate((expand_weight, shrink_weight.T), axis=1)

    parts = to_rows(
        jnp.concatenate((spread_images(tokens, block), spread_images(cotangent, block)), axis=2)
    )
    input_parts = cross(parts[:, :block], jnp.broadcast_to(small[None], (ny,) + small.shape))
    input_parts, grad_parts, units_weight, weight_out = together(
        input_parts, parts[:, block:], units_weight, project_out.T
    )
    input_parts, small = input_parts[:, :block], input_parts[:, block : block + 24]
    grad_parts = cross(grad_parts)
    weight_out = gather_weight(weight_out)
    units_weight = lax.all_gather(units_weight, "gy", axis=0, tiled=True)
    small = small.astype(WIDE)
    small = small[:, :8] + (small[:, 8:16] + small[:, 16:])
    out_shift, attn_scale, gain_one, shift_one, gain_two, shift_two, shrink_shift, ff_scale = [
        small[:, k].reshape(D) for k in range(8)
    ]
    inputs = join_width(input_parts).astype(WIDE)

    first, first_hat, first_rstd = norm_forward(inputs, gain_one, shift_one)
    first_near = gather_step(first)
    first_other = swap(first_near, "gx", 1)
    first_all = jnp.concatenate((first_near, first_other), axis=0)
    mixed = lax.dot_general(
        weight_in, first_all, (((0,), (1,)), ((), ())), preferred_element_type=WIDE
    )
    query = (mixed[:head_cols] + query_bias[:, None]).astype(LOW)
    keys = mixed[head_cols : 2 * head_cols].astype(LOW)
    values = (mixed[2 * head_cols :] + value_bias[:, None]).astype(LOW)
    heads = head_cols // HEAD_DIM
    half = attend_forward(query, keys, values, mask, ones, 0, heads // 2)
    *half, grad_parts = together(*half, grad_parts)
    grad = join_width(grad_parts).astype(WIDE)
    grad_b = grad * ff_scale
    grad_b_own, grad_b_other = gather_far(grad_b.astype(LOW))
    attended, attended_wide, log_total = attend_forward(
        query, keys, values, mask, ones, heads // 2, heads - heads // 2, half
    )
    attended, grad_b_other = together(attended, grad_b_other)
    grad_b_near = jnp.concatenate((grad_b_own, grad_b_other), axis=0)
    grad_b_far = swap(grad_b_near, "gx", 1)

    kept, sent = project_rows(attended, weight_out)
    branch_a = scatter_far(scatter_near(kept, sent)) + out_shift
    middle = inputs + attn_scale * branch_a
    second, second_hat, second_rstd = norm_forward(middle, gain_two, shift_two)
    second_near, second_far = gather_halves(second)
    hidden, slope, kept_b, sent_b = hidden_forward(
        second_near, second_far, units_weight, expand_bias[None]
    )
    grad_pre, kept, sent, pre_sum = hidden_backward(grad_b_near, grad_b_far, units_weight, slope)
    wide_grads = unit_grads(grad_b_near, grad_b_far, second_near, second_far, hidden, grad_pre)
    grad_second, received = scatter_last(scatter_near(kept, sent))
    received, wide_grads = together(received, wide_grads)
    grad_second = grad_second + received.astype(WIDE)
    wide_grads = lax.psum_scatter(wide_grads, "gy", scatter_dimension=0, tiled=True)

    grad_middle = grad + norm_backward(grad_second, gain_two, second_hat, second_rstd)
    grad_a = grad_middle * attn_scale
    grad_a_own, grad_a_other = gather_far(grad_a.astype(LOW))
    branch_near = scatter_near(kept_b, sent_b)
    grad_a_other, branch_near = together(grad_a_other, branch_near)
    grad_a_near = jnp.concatenate((grad_a_own, grad_a_other), axis=0)
    grad_a_other = swap(grad_a_near, "gx", 1)
    grad_a_all = jnp.concatenate((grad_a_near, grad_a_other), axis=0)
    branch_kept, branch_far = scatter_last(branch_near)
    grad_attended = lax.dot_general(
        weight_out, grad_a_all, (((0,), (1,)), ((), ())), preferred_element_type=WIDE
    ).astype(LOW)
    half = attend_backward(
        query, keys, values, grad_attended, attended_wide, log_total, mask, ones, 0, heads // 2
    )
    half, branch_far = together(half, branch_far)
    grad_mixed = attend_backward(
        query,
        keys,
        values,
        grad_attended,
        attended_wide,
        log_total,
        mask,
        ones,
        heads // 2,
        heads - heads // 2,
        (half,),
    )
    branch_b = branch_kept + branch_far.astype(WIDE) + shrink_shift
    output_parts = cut_width((middle + ff_scale * branch_b).astype(LOW))
    joined = grad_mixed.reshape(3 * head_cols, nx * block)
    kept, sent = project_rows(joined, weight_in)
    shares = (first_near, first_other, grad_a_near, grad_a_other, joined, attended)
    received, head_sent, output_parts = together(
        swap(sent, "gx", 1), head_grads_of(*shares, True), output_parts
    )
    grad_first, received = scatter_last(kept + received.astype(WIDE))
    received, head_other, head_kept, wide_grads = together(
        received, swap(head_sent, "gy", 1), head_grads_of(*shares, False), wide_grads
    )
    grad_first = grad_first + received.astype(WIDE)
    wide_grads = wide_grads.astype(WIDE)
    head_kept, head_other = scatter_step(head_kept + head_other.astype(WIDE), 2)
    input_gradient = grad_middle + norm_backward(grad_first, gain_one, first_hat, first_rstd)
    sums = jnp.stack(
        [
            jnp.sum(item, axis=0)
            for item in (
                grad_a,
                grad_middle * branch_a,
                grad_first * first_hat,
                grad_first,
                grad_second * second_hat,
                grad_second,
                grad_b,
                grad * branch_b,
            )
        ]
    )
    image_sums = jnp.concatenate(
        (
            jnp.sum(grad_mixed[0].astype(WIDE), axis=1),
            jnp.sum(grad_mixed[2].astype(WIDE), axis=1),
            pre_sum[0],
        )
    )
    input_parts = cut_width(input_gradient.astype(LOW))
    input_parts, output_parts = together(input_parts, cross(output_parts))
    input_parts = cross(input_parts, split_lines(sums), spread_lines(image_sums))
    input_parts, head_other = together(input_parts, head_other)
    head_grads = head_kept + head_other.astype(WIDE)
    bit = 4
    while bit < ny:
        head_kept, head_other = scatter_step(head_grads, bit)
        head_grads = head_kept + head_other.astype(WIDE)
        bit *= 2
    block_output = join_images(trade_images(output_parts), packed_shape)
    input_gradient = join_images(to_images(input_parts[:, :block]), packed_shape).astype(WIDE)
    sums = over_rows(sum_lines(input_parts[:, block : block + 16]))
    lines = 2 * image_sums.shape[0] * ny // D
    image_sums = sum_lines(input_parts[:, block + 16 : block + 16 + lines]).reshape(-1)
    head_sums, pre_sum = image_sums[: 2 * head_cols], image_sums[2 * head_cols :]
    return (
        block_output,
        input_gradient,
        head_grads[:, : 3 * head_cols].reshape(-1, 3, head_cols),
        head_sums[:head_cols],
        head_sums[head_cols:],
        head_grads[:, 3 * head_cols :].T,
        sums[0],
        sums[1],
        sums[2],
        sums[3],
        sums[4],
        sums[5],
        wide_grads[:, hidden_cols:],
        pre_sum,
        wide_grads[:, :hidden_cols].T,
        sums[6],
        sums[7],
    )


def solution(mesh):
    rows = P("gx", "gy", None)
    wide, heads = P("gy"), P("gx")
    placed = (
        rows, P("gy", None, "gx"), heads, heads, P("gx", "gy"), wide, wide, wide, wide, wide, wide,
        P("gy", "gx"), heads, P("gx", "gy"), wide, wide, rows,
    )
    results = (
        rows, rows, P("gy", None, "gx"), heads, heads, P("gx", "gy"), wide, wide, wide, wide, wide,
        wide, P("gy", "gx"), heads, P("gx", "gy"), wide, wide,
    )
    return jax.shard_map(
        on_device, mesh=mesh, in_specs=placed, out_specs=results, check_vma=False
    )
```

```python
import math

import jax
import jax.numpy as jnp
from jax import lax
from jax.experimental import pallas as pl
from jax.experimental.pallas import tpu as pltpu
from jax.sharding import PartitionSpec as P

D = 1024
HEAD_DIM = 64
SEQ = 1370
SCALE = HEAD_DIM ** (-0.5)
LOW = jnp.bfloat16
WIDE = jnp.float32


def swap(values, axis, bit):
    size = lax.axis_size(axis)
    return lax.ppermute(values, axis, [(k, k ^ bit) for k in range(size)])


def together(*values):
    return lax.optimization_barrier(values)


def gather_far(values):
    bit = lax.axis_size("gx") // 2
    while bit > 2:
        values = jnp.concatenate((values, swap(values, "gx", bit)), axis=0)
        bit //= 2
    return values, swap(values, "gx", 2)


def gather_step(values):
    return jnp.concatenate(gather_far(values), axis=0)


def gather_halves(values):
    near = gather_step(values)
    return near, swap(near, "gx", 1)


def slot_blocks(count):
    order = [0]
    bit = count // 2
    while bit:
        order = order + [k ^ bit for k in order]
        bit //= 2
    return order


def scatter_near(kept, sent):
    return kept + swap(sent, "gx", 1).astype(WIDE)


def scatter_last(partial):
    bit = 2
    while True:
        half = partial.shape[0] // 2
        received = swap(partial[half:].astype(LOW), "gx", bit)
        partial = partial[:half]
        bit *= 2
        if bit >= lax.axis_size("gx"):
            return partial, received
        partial = partial + received.astype(WIDE)


def scatter_far(partial):
    kept, received = scatter_last(partial)
    return kept + received.astype(WIDE)


def scatter_step(total, bit):
    half = total.shape[0] // 2
    return total[:half], swap(total[half:].astype(LOW), "gy", bit)


def pieces(values, count):
    parts = []
    for _ in range(count):
        head = lax.reduce_precision(values, exponent_bits=8, mantissa_bits=7)
        parts.append(head.astype(LOW))
        values = values - head
    return parts


def spread_images(values, block):
    nx, ny = lax.axis_size("gx"), lax.axis_size("gy")
    images = values.reshape(ny // nx, SEQ, D // ny)
    images = jnp.pad(images, ((0, 0), (0, nx * block - SEQ), (0, 0)))
    return images.reshape(ny // nx, nx, block, D // ny).transpose(1, 0, 2, 3)


def to_rows(parts):
    parts = lax.all_to_all(parts, "gx", split_axis=0, concat_axis=0, tiled=True)
    return parts.reshape((-1,) + parts.shape[2:])


def to_images(parts):
    nx, ny = lax.axis_size("gx"), lax.axis_size("gy")
    parts = parts.reshape((nx, ny // nx) + parts.shape[1:])
    return lax.all_to_all(parts, "gx", split_axis=0, concat_axis=0, tiled=True)


def trade_images(parts):
    nx, ny = lax.axis_size("gx"), lax.axis_size("gy")
    place = lax.axis_index("gx")
    shape = (nx, ny // nx) + parts.shape[1:]
    bit = 1
    while bit < nx:
        pair = parts.reshape((nx // (2 * bit), 2, bit) + shape[1:])
        upper = (place & bit) != 0
        mine = jnp.where(upper, pair[:, 1], pair[:, 0])
        theirs = swap(jnp.where(upper, pair[:, 0], pair[:, 1]), "gx", bit)
        low, high = jnp.where(upper, theirs, mine), jnp.where(upper, mine, theirs)
        parts = jnp.stack((low, high), axis=1).reshape(shape)
        bit *= 2
    return parts


def join_images(parts, packed_shape):
    nx, per, block, width = parts.shape
    parts = parts.transpose(1, 0, 2, 3).reshape(per, nx * block, width)
    return parts[:, :SEQ].reshape(packed_shape)


def over_rows(sums):
    bit = 1
    while bit < lax.axis_size("gx"):
        sums = sums + swap(sums, "gx", bit)
        bit *= 2
    return sums


def cross(parts, *extra):
    if extra:
        rows = sum(item.shape[1] for item in extra)
        space = jnp.zeros((parts.shape[0], -rows % 16, parts.shape[2]), LOW)
        parts = jnp.concatenate((parts, *extra, space), axis=1)
    return lax.all_to_all(parts, "gy", split_axis=0, concat_axis=0, tiled=True)


def spread_lines(values):
    ny = lax.axis_size("gy")
    lines = jnp.concatenate([item.reshape(-1, D // ny) for item in pieces(values, 2)], axis=0)
    return jnp.broadcast_to(lines[None], (ny,) + lines.shape)


def split_lines(vectors):
    ny = lax.axis_size("gy")
    lines = jnp.concatenate(pieces(vectors, 2), axis=0)
    return lines.reshape(-1, ny, D // ny).transpose(1, 0, 2)


def sum_lines(lines):
    return jnp.sum(lines.astype(WIDE), axis=0).reshape(2, -1, lines.shape[2]).sum(axis=0)


def join_width(parts):
    return parts.transpose(1, 0, 2).reshape(parts.shape[1], D)


def cut_width(values):
    ny = lax.axis_size("gy")
    return values.reshape(values.shape[0], ny, D // ny).transpose(1, 0, 2)


def gather_weight(weight):
    place = lax.axis_index("gy")
    rows, cols = weight.shape
    weight = weight[None]
    bit = lax.axis_size("gy") // 2
    while bit:
        other = swap(weight, "gy", bit)
        upper = (place & bit) != 0
        low, high = jnp.where(upper, other, weight), jnp.where(upper, weight, other)
        weight = jnp.stack((low, high), axis=1).reshape(-1, rows, cols)
        bit //= 2
    return weight.reshape(-1, cols)


def norm_forward(values, gain, shift):
    center = jnp.mean(values, axis=1, keepdims=True)
    spread = jnp.mean(values * values, axis=1, keepdims=True) - center * center
    rstd = lax.rsqrt(spread + 1e-06)
    normed = (values - center) * rstd
    return (normed * gain + shift).astype(LOW), normed, rstd


def norm_backward(grad, gain, normed, rstd):
    scaled = grad * gain
    total = jnp.mean(scaled, axis=1, keepdims=True)
    along = jnp.mean(scaled * normed, axis=1, keepdims=True)
    return rstd * (scaled - total - normed * along)


def times(left, right):
    return jnp.dot(left, right, preferred_element_type=WIDE)


def times_t(left, right):
    return lax.dot_general(left, right, (((1,), (1,)), ((), ())), preferred_element_type=WIDE)


def inner_rows(left, right):
    return lax.dot_general(left, right, (((0,), (0,)), ((), ())), preferred_element_type=WIDE)


def lane_blocks(size):
    return [(start, min(256, size - start)) for start in range(0, size, 256)]


def with_row(head, row):
    return jnp.concatenate((head, row), axis=0)


def attend_forward_body(q_ref, k_ref, v_ref, mask_ref, ones_ref, *refs):
    low_ref, wide_ref, log_ref = refs[-3:]
    keys = with_row(k_ref[...], mask_ref[...]).T
    query = with_row((q_ref[...].astype(WIDE) * SCALE).astype(LOW), ones_ref[...])
    values = with_row(v_ref[...], ones_ref[...])
    for start, size in lane_blocks(query.shape[1]):
        lanes = slice(start, start + size)
        scores = jnp.dot(keys, query[:, lanes], preferred_element_type=WIDE)
        peak = jnp.max(scores, axis=0, keepdims=True)
        raised = jnp.exp(scores - peak).astype(LOW)
        mixed = jnp.dot(values, raised, preferred_element_type=WIDE)
        total = mixed[HEAD_DIM : HEAD_DIM + 1]
        attended = mixed[:HEAD_DIM] / total
        wide_ref[:, lanes] = attended
        low_ref[:, lanes] = attended.astype(LOW)
        log_ref[0, :, lanes] = peak + jnp.log(total)


def attend_forward(query, keys, values, mask, ones, first_head, count, before=()):
    cols, rows = query.shape
    heads = cols // HEAD_DIM
    head = pl.BlockSpec((HEAD_DIM, rows), lambda h: (h + first_head, 0))
    shared = pl.BlockSpec((HEAD_DIM, rows), lambda h: (0, 0))
    return pl.pallas_call(
        attend_forward_body,
        grid=(count,),
        in_specs=[head, head, head, shared, shared] + [pl.BlockSpec(memory_space=pl.ANY)] * len(before),
        out_specs=[head, head, pl.BlockSpec((1, 1, rows), lambda h: (h + first_head, 0, 0))],
        out_shape=[
            jax.ShapeDtypeStruct((cols, rows), LOW),
            jax.ShapeDtypeStruct((cols, rows), WIDE),
            jax.ShapeDtypeStruct((heads, 1, rows), WIDE),
        ],
        input_output_aliases={5 + k: k for k in range(len(before))},
        compiler_params=pltpu.CompilerParams(vmem_limit_bytes=40 * 1024 * 1024),
        cost_estimate=pl.CostEstimate(
            flops=48 * count * rows * rows * HEAD_DIM,
            bytes_accessed=12 * count * HEAD_DIM * rows,
            transcendentals=count * rows * rows,
        ),
    )(query, keys, values, mask, ones, *before)


def attend_backward_body(
    q_ref, k_ref, v_ref, g_ref, wide_ref, log_ref, mask_ref, ones_ref, *refs
):
    out_ref = refs[-1]
    rows = q_ref.shape[1]
    keys_t = k_ref[...]
    keys = with_row(keys_t, mask_ref[...]).T
    query = with_row((q_ref[...].astype(WIDE) * SCALE).astype(LOW), ones_ref[...])
    values = with_row(v_ref[...], mask_ref[...]).T[:, :HEAD_DIM]
    both = with_row(q_ref[...], g_ref[...]).T
    grad_keys = jnp.zeros((rows, HEAD_DIM), WIDE)
    grad_values = jnp.zeros((rows, HEAD_DIM), WIDE)
    for start, size in lane_blocks(rows):
        lanes = slice(start, start + size)
        grad_out = g_ref[:, lanes]
        scores = jnp.dot(keys, query[:, lanes], preferred_element_type=WIDE)
        probs = jnp.exp(scores - log_ref[0, :, lanes])
        grad_probs = jnp.dot(values, grad_out, preferred_element_type=WIDE)
        along = jnp.sum(grad_out.astype(WIDE) * wide_ref[:, lanes], axis=0, keepdims=True)
        grad_scores = (probs * (grad_probs - along)).astype(LOW)
        grad_query = jnp.dot(keys_t, grad_scores, preferred_element_type=WIDE) * SCALE
        out_ref[0, :, lanes] = grad_query.astype(LOW)
        grad_keys += jnp.dot(
            grad_scores, both[lanes, :HEAD_DIM], preferred_element_type=WIDE
        )
        grad_values += jnp.dot(
            probs.astype(LOW), both[lanes, HEAD_DIM:], preferred_element_type=WIDE
        )
    joined = jnp.concatenate((grad_keys * SCALE, grad_values), axis=1).T
    out_ref[1] = joined[:HEAD_DIM].astype(LOW)
    out_ref[2] = joined[HEAD_DIM:].astype(LOW)


def attend_backward(
    query, keys, values, grad_out, wide, log_total, mask, ones, first_head, count, before=()
):
    cols, rows = query.shape
    head = pl.BlockSpec((HEAD_DIM, rows), lambda h: (h + first_head, 0))
    shared = pl.BlockSpec((HEAD_DIM, rows), lambda h: (0, 0))
    return pl.pallas_call(
        attend_backward_body,
        grid=(count,),
        in_specs=[
            head,
            head,
            head,
            head,
            head,
            pl.BlockSpec((1, 1, rows), lambda h: (h + first_head, 0, 0)),
            shared,
            shared,
        ]
        + [pl.BlockSpec(memory_space=pl.ANY)] * len(before),
        out_specs=pl.BlockSpec((3, HEAD_DIM, rows), lambda h: (0, h + first_head, 0)),
        out_shape=jax.ShapeDtypeStruct((3, cols, rows), LOW),
        input_output_aliases={8 + k: k for k in range(len(before))},
        compiler_params=pltpu.CompilerParams(vmem_limit_bytes=40 * 1024 * 1024),
        cost_estimate=pl.CostEstimate(
            flops=56 * count * rows * rows * HEAD_DIM,
            bytes_accessed=20 * count * HEAD_DIM * rows,
            transcendentals=count * rows * rows,
        ),
    )(query, keys, values, grad_out, wide, log_total, mask, ones, *before)


def forward_body(
    near_ref, far_ref, expand_ref, shrink_ref, bias_ref, hidden_ref, slope_ref, kept_ref, sent_ref
):
    def work(rows_ref, down_ref):
        preact = jnp.dot(rows_ref[...], expand_ref[...], preferred_element_type=WIDE)
        preact = preact + bias_ref[...]
        share = 0.5 * (1.0 + lax.erf(preact * 0.5**0.5))
        hidden = (preact * share).astype(LOW)
        hidden_ref[...] = hidden
        bell = jnp.exp(preact * preact * -0.5) * (0.5 / math.pi) ** 0.5
        slope_ref[...] = share + preact * bell
        down_ref[...] = times_t(hidden, shrink_ref[...]).astype(down_ref.dtype)

    @pl.when(pl.program_id(0) < 2)
    def _():
        work(far_ref, sent_ref)

    @pl.when(pl.program_id(0) >= 2)
    def _():
        work(near_ref, kept_ref)


def backward_body(
    near_ref, far_ref, expand_ref, shrink_ref, slope_ref, pre_ref, kept_ref, sent_ref, sum_ref
):
    def work(rows_ref, back_ref):
        grad_hidden = jnp.dot(rows_ref[...], shrink_ref[...], preferred_element_type=WIDE)
        grad_pre = (grad_hidden * slope_ref[...]).astype(LOW)
        pre_ref[...] = grad_pre
        back_ref[...] = times_t(grad_pre, expand_ref[...]).astype(back_ref.dtype)
        sums = jnp.sum(grad_pre.astype(WIDE), axis=0, keepdims=True)

        @pl.when(pl.program_id(0) == 0)
        def _():
            sum_ref[...] = sums

        @pl.when(pl.program_id(0) != 0)
        def _():
            sum_ref[...] += sums

    @pl.when(pl.program_id(0) < 2)
    def _():
        work(far_ref, sent_ref)

    @pl.when(pl.program_id(0) >= 2)
    def _():
        work(near_ref, kept_ref)


def hidden_specs(rows, width, cols):
    step = rows // 2
    near = pl.BlockSpec((step, width), lambda r: (jnp.maximum(r - 2, 0), 0))
    far = pl.BlockSpec((step, width), lambda r: (jnp.minimum(r, 1), 0))
    units = pl.BlockSpec((step, cols), lambda r: ((r + 2) % 4, 0))
    expand = pl.BlockSpec((width, cols), lambda r: (0, 0))
    shrink = pl.BlockSpec((width, cols), lambda r: (0, 1))
    line = pl.BlockSpec((1, cols), lambda r: (0, 0))
    return near, far, units, expand, shrink, line


def hidden_cost(rows, width, cols):
    return pl.CostEstimate(
        flops=16 * rows * cols * width,
        bytes_accessed=10 * rows * width + 12 * rows * cols + 4 * width * cols,
        transcendentals=4 * rows * cols,
    )


def hidden_forward(near_rows, far_rows, weights, bias):
    rows, width = near_rows.shape
    cols = weights.shape[1] // 2
    near, far, units, expand, shrink, line = hidden_specs(rows, width, cols)
    return pl.pallas_call(
        forward_body,
        grid=(4,),
        in_specs=[near, far, expand, shrink, line],
        out_specs=[units, units, near, far],
        out_shape=[
            jax.ShapeDtypeStruct((2 * rows, cols), LOW),
            jax.ShapeDtypeStruct((2 * rows, cols), WIDE),
            jax.ShapeDtypeStruct((rows, width), WIDE),
            jax.ShapeDtypeStruct((rows, width), LOW),
        ],
        compiler_params=pltpu.CompilerParams(vmem_limit_bytes=40 * 1024 * 1024),
        cost_estimate=hidden_cost(rows, width, cols),
    )(near_rows, far_rows, weights, weights, bias)


def hidden_backward(near_rows, far_rows, weights, slope):
    rows, width = near_rows.shape
    cols = weights.shape[1] // 2
    near, far, units, expand, shrink, line = hidden_specs(rows, width, cols)
    return pl.pallas_call(
        backward_body,
        grid=(4,),
        in_specs=[near, far, expand, shrink, units],
        out_specs=[units, near, far, line],
        out_shape=[
            jax.ShapeDtypeStruct((2 * rows, cols), LOW),
            jax.ShapeDtypeStruct((rows, width), WIDE),
            jax.ShapeDtypeStruct((rows, width), LOW),
            jax.ShapeDtypeStruct((1, cols), WIDE),
        ],
        compiler_params=pltpu.CompilerParams(vmem_limit_bytes=40 * 1024 * 1024),
        cost_estimate=hidden_cost(rows, width, cols),
    )(near_rows, far_rows, weights, weights, slope)


def turned_slot(slot, count):
    turned = slot * 0
    while count > 1:
        turned = turned * 2 + slot % 2
        slot = slot // 2
        count //= 2
    return turned


def far_first(total, tiles):
    order = jnp.array([turned_slot(slot, tiles) for slot in range(tiles)])
    parts = total.reshape(tiles, -1, total.shape[1])
    parts = jnp.take(parts, order ^ lax.axis_index("gy"), axis=0).reshape(total.shape)
    half = total.shape[0] // 2
    return parts[:half], parts[half:].astype(LOW)


def unit_grads_body(
    gn_ref, gf_ref, sn_ref, sf_ref, hidden_ref, pre_ref, out_ref
):
    half = gn_ref.shape[0]

    def work(near_ref, far_ref, units_ref):
        total = inner_rows(near_ref[...], units_ref[:half])
        total += inner_rows(far_ref[...], units_ref[half:])
        out_ref[...] = total.astype(LOW)

    @pl.when(pl.program_id(0) < 4)
    def _():
        work(gn_ref, gf_ref, hidden_ref)

    @pl.when(pl.program_id(0) >= 4)
    def _():
        work(sn_ref, sf_ref, pre_ref)


def unit_grads(grad_near, grad_far, second_near, second_far, hidden, grad_pre):
    half, width = grad_near.shape
    rows, cols = hidden.shape
    tile = width // 4
    early = pl.BlockSpec((half, tile), lambda r: (0, jnp.minimum(r, 3)))
    late = pl.BlockSpec((half, tile), lambda r: (0, jnp.maximum(r - 4, 0)))
    whole = pl.BlockSpec((rows, cols), lambda r: (0, 0))
    return pl.pallas_call(
        unit_grads_body,
        grid=(8,),
        in_specs=[early, early, late, late, whole, whole],
        out_specs=pl.BlockSpec((tile, cols), lambda r: (r % 4, r // 4)),
        out_shape=jax.ShapeDtypeStruct((width, 2 * cols), LOW),
        compiler_params=pltpu.CompilerParams(vmem_limit_bytes=40 * 1024 * 1024),
        cost_estimate=pl.CostEstimate(
            flops=8 * rows * cols * width,
            bytes_accessed=4 * rows * (width + cols) + 4 * width * cols,
            transcendentals=0,
        ),
    )(grad_near, grad_far, second_near, second_far, hidden, grad_pre)


def project_body(rows_ref, weight_ref, kept_ref, sent_ref, turned_ref):
    @pl.when(pl.program_id(0) == 0)
    def _():
        turned_ref[...] = rows_ref[...].T

    total = times_t(turned_ref[...], weight_ref[...])
    half = kept_ref.shape[0]
    kept_ref[...] = total[:half]
    sent_ref[...] = total[half:].astype(LOW)


def project_rows(values, weight):
    cols, rows = values.shape
    width = weight.shape[0]
    tile = width // 4
    return pl.pallas_call(
        project_body,
        grid=(4,),
        in_specs=[
            pl.BlockSpec((cols, rows), lambda t: (0, 0)),
            pl.BlockSpec((tile, cols), lambda t: (t, 0)),
        ],
        out_specs=[
            pl.BlockSpec((rows // 2, tile), lambda t: (0, t)),
            pl.BlockSpec((rows // 2, tile), lambda t: (0, t)),
        ],
        out_shape=[
            jax.ShapeDtypeStruct((rows // 2, width), WIDE),
            jax.ShapeDtypeStruct((rows // 2, width), LOW),
        ],
        scratch_shapes=[pltpu.VMEM((rows, cols), LOW)],
        compiler_params=pltpu.CompilerParams(vmem_limit_bytes=40 * 1024 * 1024),
        cost_estimate=pl.CostEstimate(
            flops=2 * rows * cols * width,
            bytes_accessed=2 * rows * cols + 2 * width * cols + 3 * rows * width,
            transcendentals=0,
        ),
    )(values, weight)


def head_grads_body(place_ref, fn_ref, ff_ref, gn_ref, gf_ref, mixed_ref, attended_ref, out_ref):
    cols = mixed_ref.shape[0]
    first = jnp.concatenate((fn_ref[...], ff_ref[...]), axis=0)
    grad = jnp.concatenate((gn_ref[...], gf_ref[...]), axis=0)
    out_ref[:, :cols] = times(mixed_ref[...], first).T.astype(out_ref.dtype)
    out_ref[:, cols:] = times(attended_ref[...], grad).T.astype(out_ref.dtype)


def head_grads_of(first_near, first_far, grad_near, grad_far, mixed, attended, upper):
    half, width = first_near.shape
    rows = 2 * half
    cols, more = mixed.shape[0], attended.shape[0]
    tiles = lax.axis_size("gy")
    tile = width // tiles
    dtype = LOW if upper else WIDE
    if tile % 128:
        first = jnp.concatenate((first_near, first_far), axis=0)
        grad = jnp.concatenate((grad_near, grad_far), axis=0)
        total = jnp.concatenate((times(mixed, first).T, times(attended, grad).T), axis=1)
        return far_first(total, tiles)[1 if upper else 0].astype(dtype)
    start = tiles // 2 if upper else 0

    def block(r, place):
        return turned_slot(r + start, tiles) ^ place[0]

    narrow = pl.BlockSpec((half, tile), lambda r, place: (0, block(r, place)))
    return pl.pallas_call(
        head_grads_body,
        grid_spec=pltpu.PrefetchScalarGridSpec(
            num_scalar_prefetch=1,
            grid=(tiles // 2,),
            in_specs=[
                narrow,
                narrow,
                narrow,
                narrow,
                pl.BlockSpec((cols, rows), lambda r, place: (0, 0)),
                pl.BlockSpec((more, rows), lambda r, place: (0, 0)),
            ],
            out_specs=pl.BlockSpec((tile, cols + more), lambda r, place: (r, 0)),
        ),
        out_shape=jax.ShapeDtypeStruct((width // 2, cols + more), dtype),
        compiler_params=pltpu.CompilerParams(vmem_limit_bytes=40 * 1024 * 1024),
        cost_estimate=pl.CostEstimate(
            flops=2 * rows * (cols + more) * width,
            bytes_accessed=2 * rows * (width + cols + more) + 2 * width * (cols + more),
            transcendentals=0,
        ),
    )(
        lax.axis_index("gy").astype(jnp.int32)[None],
        first_near,
        first_far,
        grad_near,
        grad_far,
        mixed,
        attended,
    )


def on_device(
    tokens,
    project_in,
    query_bias,
    value_bias,
    project_out,
    output_bias,
    attention_scale,
    first_norm_gain,
    first_norm_bias,
    second_norm_gain,
    second_norm_bias,
    expand_weight,
    expand_bias,
    shrink_weight,
    shrink_bias,
    feedforward_scale,
    cotangent,
):
    nx, ny = lax.axis_size("gx"), lax.axis_size("gy")
    head_cols = project_out.shape[0]
    hidden_cols = expand_weight.shape[1]
    packed_shape = tokens.shape
    block = -(-SEQ // (nx * 16)) * 16
    column = jnp.arange(block)
    mask = jnp.concatenate(
        [
            jnp.where((lax.axis_index("gx") ^ k) * block + column < SEQ, 0.0, -1e30)
            for k in slot_blocks(nx)
        ]
    )
    top = jnp.arange(HEAD_DIM)[:, None] == 0
    mask = jnp.where(top, mask[None], 0.0).astype(LOW)
    ones = jnp.where(top, jnp.ones((1, nx * block), WIDE), 0.0).astype(LOW)

    small = jnp.concatenate(
        pieces(
            jnp.stack(
                (
                    output_bias,
                    attention_scale,
                    first_norm_gain,
                    first_norm_bias,
                    second_norm_gain,
                    second_norm_bias,
                    shrink_bias,
                    feedforward_scale,
                )
            ),
            3,
        ),
        axis=0,
    )
    weight_in = lax.all_gather(project_in.reshape(-1, 3 * head_cols), "gy", axis=0, tiled=True)
    units_weight = jnp.concatenate((expand_weight, shrink_weight.T), axis=1)

    parts = to_rows(
        jnp.concatenate((spread_images(tokens, block), spread_images(cotangent, block)), axis=2)
    )
    input_parts = cross(parts[:, :block], jnp.broadcast_to(small[None], (ny,) + small.shape))
    input_parts, grad_parts, units_weight, weight_out = together(
        input_parts, parts[:, block:], units_weight, project_out.T
    )
    input_parts, small = input_parts[:, :block], input_parts[:, block : block + 24]
    grad_parts = cross(grad_parts)
    weight_out = gather_weight(weight_out)
    units_weight = lax.all_gather(units_weight, "gy", axis=0, tiled=True)
    small = small.astype(WIDE)
    small = small[:, :8] + (small[:, 8:16] + small[:, 16:])
    out_shift, attn_scale, gain_one, shift_one, gain_two, shift_two, shrink_shift, ff_scale = [
        small[:, k].reshape(D) for k in range(8)
    ]
    inputs = join_width(input_parts).astype(WIDE)

    first, first_hat, first_rstd = norm_forward(inputs, gain_one, shift_one)
    first_near = gather_step(first)
    first_other = swap(first_near, "gx", 1)
    first_all = jnp.concatenate((first_near, first_other), axis=0)
    mixed = lax.dot_general(
        weight_in, first_all, (((0,), (1,)), ((), ())), preferred_element_type=WIDE
    )
    query = (mixed[:head_cols] + query_bias[:, None]).astype(LOW)
    keys = mixed[head_cols : 2 * head_cols].astype(LOW)
    values = (mixed[2 * head_cols :] + value_bias[:, None]).astype(LOW)
    heads = head_cols // HEAD_DIM
    half = attend_forward(query, keys, values, mask, ones, 0, heads // 2)
    *half, grad_parts = together(*half, grad_parts)
    grad = join_width(grad_parts).astype(WIDE)
    grad_b = grad * ff_scale
    grad_b_own, grad_b_other = gather_far(grad_b.astype(LOW))
    attended, attended_wide, log_total = attend_forward(
        query, keys, values, mask, ones, heads // 2, heads - heads // 2, half
    )
    attended, grad_b_other = together(attended, grad_b_other)
    grad_b_near = jnp.concatenate((grad_b_own, grad_b_other), axis=0)
    grad_b_far = swap(grad_b_near, "gx", 1)

    kept, sent = project_rows(attended, weight_out)
    branch_a = scatter_far(scatter_near(kept, sent)) + out_shift
    middle = inputs + attn_scale * branch_a
    second, second_hat, second_rstd = norm_forward(middle, gain_two, shift_two)
    second_near, second_far = gather_halves(second)
    hidden, slope, kept_b, sent_b = hidden_forward(
        second_near, second_far, units_weight, expand_bias[None]
    )
    grad_pre, kept, sent, pre_sum = hidden_backward(grad_b_near, grad_b_far, units_weight, slope)
    wide_grads = unit_grads(grad_b_near, grad_b_far, second_near, second_far, hidden, grad_pre)
    grad_second, received = scatter_last(scatter_near(kept, sent))
    received, wide_grads = together(received, wide_grads)
    grad_second = grad_second + received.astype(WIDE)
    wide_grads = lax.psum_scatter(wide_grads, "gy", scatter_dimension=0, tiled=True)

    grad_middle = grad + norm_backward(grad_second, gain_two, second_hat, second_rstd)
    grad_a = grad_middle * attn_scale
    grad_a_own, grad_a_other = gather_far(grad_a.astype(LOW))
    branch_near = scatter_near(kept_b, sent_b)
    grad_a_other, branch_near = together(grad_a_other, branch_near)
    grad_a_near = jnp.concatenate((grad_a_own, grad_a_other), axis=0)
    grad_a_other = swap(grad_a_near, "gx", 1)
    grad_a_all = jnp.concatenate((grad_a_near, grad_a_other), axis=0)
    branch_kept, branch_far = scatter_last(branch_near)
    grad_attended = lax.dot_general(
        weight_out, grad_a_all, (((0,), (1,)), ((), ())), preferred_element_type=WIDE
    ).astype(LOW)
    grad_mixed = attend_backward(
        query, keys, values, grad_attended, attended_wide, log_total, mask, ones, 0, heads
    )
    grad_mixed, branch_far = together(grad_mixed, branch_far)
    branch_b = branch_kept + branch_far.astype(WIDE) + shrink_shift
    output_parts = cut_width((middle + ff_scale * branch_b).astype(LOW))
    joined = grad_mixed.reshape(3 * head_cols, nx * block)
    kept, sent = project_rows(joined, weight_in)
    shares = (first_near, first_other, grad_a_near, grad_a_other, joined, attended)
    received, head_sent, output_parts = together(
        swap(sent, "gx", 1), head_grads_of(*shares, True), output_parts
    )
    grad_first, received = scatter_last(kept + received.astype(WIDE))
    received, head_other, head_kept, wide_grads = together(
        received, swap(head_sent, "gy", 1), head_grads_of(*shares, False), wide_grads
    )
    grad_first = grad_first + received.astype(WIDE)
    wide_grads = wide_grads.astype(WIDE)
    head_kept, head_other = scatter_step(head_kept + head_other.astype(WIDE), 2)
    input_gradient = grad_middle + norm_backward(grad_first, gain_one, first_hat, first_rstd)
    sums = jnp.stack(
        [
            jnp.sum(item, axis=0)
            for item in (
                grad_a,
                grad_middle * branch_a,
                grad_first * first_hat,
                grad_first,
                grad_second * second_hat,
                grad_second,
                grad_b,
                grad * branch_b,
            )
        ]
    )
    image_sums = jnp.concatenate(
        (
            jnp.sum(grad_mixed[0].astype(WIDE), axis=1),
            jnp.sum(grad_mixed[2].astype(WIDE), axis=1),
            pre_sum[0],
        )
    )
    input_parts = cut_width(input_gradient.astype(LOW))
    input_parts, output_parts = together(input_parts, cross(output_parts))
    input_parts = cross(input_parts, split_lines(sums), spread_lines(image_sums))
    input_parts, head_other = together(input_parts, head_other)
    head_grads = head_kept + head_other.astype(WIDE)
    bit = 4
    while bit < ny:
        head_kept, head_other = scatter_step(head_grads, bit)
        head_grads = head_kept + head_other.astype(WIDE)
        bit *= 2
    block_output = join_images(trade_images(output_parts), packed_shape)
    input_gradient = join_images(to_images(input_parts[:, :block]), packed_shape).astype(WIDE)
    sums = over_rows(sum_lines(input_parts[:, block : block + 16]))
    lines = 2 * image_sums.shape[0] * ny // D
    image_sums = sum_lines(input_parts[:, block + 16 : block + 16 + lines]).reshape(-1)
    head_sums, pre_sum = image_sums[: 2 * head_cols], image_sums[2 * head_cols :]
    return (
        block_output,
        input_gradient,
        head_grads[:, : 3 * head_cols].reshape(-1, 3, head_cols),
        head_sums[:head_cols],
        head_sums[head_cols:],
        head_grads[:, 3 * head_cols :].T,
        sums[0],
        sums[1],
        sums[2],
        sums[3],
        sums[4],
        sums[5],
        wide_grads[:, hidden_cols:],
        pre_sum,
        wide_grads[:, :hidden_cols].T,
        sums[6],
        sums[7],
    )


def solution(mesh):
    rows = P("gx", "gy", None)
    wide, heads = P("gy"), P("gx")
    placed = (
        rows, P("gy", None, "gx"), heads, heads, P("gx", "gy"), wide, wide, wide, wide, wide, wide,
        P("gy", "gx"), heads, P("gx", "gy"), wide, wide, rows,
    )
    results = (
        rows, rows, P("gy", None, "gx"), heads, heads, P("gx", "gy"), wide, wide, wide, wide, wide,
        wide, P("gy", "gx"), heads, P("gx", "gy"), wide, wide,
    )
    return jax.shard_map(
        on_device, mesh=mesh, in_specs=placed, out_specs=results, check_vma=False
    )
```
